256 devices in a mesh: dom: 64 (over y_hi, z, x), rep: 4 (over y_lo, core).
Axes of the slice: x: 4, y: 4 (y_hi: 2, y_lo: 2; y = y_hi * 2 + y_lo), z: 8, core: 2. Of those that a mesh axis runs over, the one named last changes fastest.
Arguments:
- entity_table: float32 [262144, 400], P('dom'), may hold values from -2.5 to 2.5
- entity_state: float32 [262144], P('dom'), may hold values from 0.02 to 0.2
- relation_table: float32 [1300, 400], replicated, may hold values from -1 to 1
- relation_state: float32 [1300], replicated, may hold values from 1 to 10
- source_rows: int32 [2, 64, 1024], P(None, 'dom', 'rep'), may hold values from 0 to 4095
- target_rows: int32 [2, 64, 1024], P(None, 'dom', 'rep'), may hold values from 0 to 4095
- relation_ids: int32 [2, 64, 1024], P(None, 'dom', 'rep'), may hold values from 0 to 1299
- live_counts: int32 [2, 64, 4], P(None, 'dom', 'rep'), may hold values from 64 to 256, as said below
Outputs:
- new_entities: float32 [262144, 400], P(('dom', 'rep'))
- new_entity_state: float32 [262144], P(('dom', 'rep'))
- new_relations: float32 [1300, 400], replicated
- new_relation_state: float32 [1300], replicated
The draws below stay inside these ranges and needn't reach their ends.
Inputs may be any that keep to these rules, and one draw needn't show every extreme that they name: live_counts[t, p, c]: live slots, the first ones, of block c of bucket p in round t; in each round some block has all 256 live.
All inputs are finite; a program needn't handle non-finite values.
Results may differ from the reference program's by a relative error of at most 0.0048.
Values may be sent and summed in bfloat16 or wider, within the bound.
A program may use at most 128 MiB of HBM per device.

```python
import math
import jax
import jax.numpy as jnp
import numpy as np
from jax import lax

W = 400
RELS = 1300
ROWS_DEV = 4096
GROUP = 256
ENTITIES = 262144
BUCKET = 1024
N_DOM = 64
N_REP = 4


def draw_live_counts(key, part):
    key = jax.random.fold_in(key, 11)
    key_base, key_dom, key_rep = jax.random.split(key, 3)
    base_counts = jax.random.randint(key_base, (2, N_DOM, N_REP), GROUP // 4, GROUP + 1)
    dom_pick = jax.random.randint(key_dom, (2,), 0, N_DOM)
    rep_pick = jax.random.randint(key_rep, (2,), 0, N_REP)
    return base_counts.at[jnp.arange(2), dom_pick, rep_pick].set(GROUP).astype(jnp.int32)


def place_ends(drawn, own_key, smallest, high):
    spot = [jax.random.randint(jax.random.fold_in(own_key, axis), (), 0, length) for axis, length in enumerate(drawn.shape)]
    widest = drawn.shape.index(max(drawn.shape))
    beside = spot[:widest] + [(spot[widest] + 1) % drawn.shape[widest]] + spot[widest + 1:]
    return drawn.at[tuple(spot)].set(smallest).at[tuple(beside)].set(high)


def block_levels(key, extent, shards, smallest, top_value):
    def one(position, parts):
        draws = jax.random.uniform(jax.random.fold_in(jax.random.fold_in(key, 6), position), (parts,), jnp.float32, smallest / len(shards), top_value / len(shards))
        return jnp.repeat(jnp.exp(draws), extent[position] // parts).reshape((-1,) + (1,) * (len(extent) - position - 1))

    loudness = one(*shards[0])
    for cut in shards[1:]:
        loudness = loudness * one(*cut)
    return loudness


def cumulative_ranks(number_of, slope):
    portions = [(1 << 20) // math.isqrt(rank ** slope) + 1 for rank in range(1, number_of + 1)]
    width = 1 + sum(portions) // (1 << 30)
    return np.cumsum(np.array([max(1, weight // width) for weight in portions]))


def ranked_ids(rng, extent, amount, slope):
    table = cumulative_ranks(amount, slope)
    ticket = jax.random.randint(jax.random.fold_in(rng, 1), extent, 0, int(table[amount - 1]))
    grade = jnp.searchsorted(jnp.asarray(table, jnp.int32), ticket, side="right")
    return jax.random.permutation(jax.random.fold_in(rng, 2), amount)[grade].astype(jnp.int32)


def scatter_about(own_key, shape, spread, limit, cuts=(), kind=jnp.bfloat16):
    entries = spread * jax.random.normal(own_key, shape, jnp.float32)
    if cuts:
        entries = entries * block_levels(own_key, shape, cuts, -0.22, 0.18)
    return jnp.clip(entries, -limit, limit).astype(kind)


def setup_inputs(seed: int = 0) -> dict:
    seeds = jax.random.split(jax.random.key(seed), 9)
    return {
        "entity_table": scatter_about(seeds[0], (ENTITIES, W), 0.35, 2.5, ((0, 64),), jnp.float32),
        "entity_state": jnp.clip(jnp.exp(math.log(0.2) - 2.3025851 * jax.random.uniform(seeds[1], (ENTITIES,), jnp.float32) ** block_levels(seeds[1], (ENTITIES,), ((0, 64),), -0.2, 0.2)), 0.02, 0.2),
        "relation_table": jnp.clip(jax.random.uniform(seeds[2], (RELS, W), jnp.float32, -1.0, 1.0), -1.0, 1.0),
        "relation_state": jnp.clip(jnp.exp(jax.random.uniform(seeds[3], (RELS,), jnp.float32, math.log(1.0), math.log(10.0))), 1.0, 10.0),
        "source_rows": place_ends(jax.random.randint(seeds[4], (2, N_DOM, BUCKET), 0, ROWS_DEV), jax.random.fold_in(seeds[4], 1), 0, ROWS_DEV - 1).astype(jnp.int32),
        "target_rows": place_ends(jax.random.randint(seeds[5], (2, N_DOM, BUCKET), 0, ROWS_DEV), jax.random.fold_in(seeds[5], 1), 0, ROWS_DEV - 1).astype(jnp.int32),
        "relation_ids": place_ends(ranked_ids(seeds[6], (2, N_DOM, BUCKET), RELS, 2), jax.random.fold_in(seeds[6], 3), 0, RELS - 1).astype(jnp.int32),
        "live_counts": draw_live_counts(jax.random.fold_in(seeds[8], 71), 0),
    }


learning_rate = 0.2
epsilon = 1e-06

def lookup(indices, table_b):
    return jnp.take(table_b, indices.astype(jnp.int32), axis=0)

def spread_rows(indices, row_count, values):
    return jax.ops.segment_sum(values.astype(jnp.float32), indices.astype(jnp.int32), num_segments=row_count)

def group_terms(sources, relations, targets, live_count):
    half_width = sources.shape[1] // 2
    src_f = sources.astype(jnp.float32)
    rel_f = relations.astype(jnp.float32)
    src_re, src_im = (src_f[:, :half_width], src_f[:, half_width:])
    rel_re, rel_im = (rel_f[:, :half_width], rel_f[:, half_width:])
    queries = jnp.concatenate([src_re * rel_re - src_im * rel_im, src_re * rel_im + src_im * rel_re], axis=1).astype(jnp.bfloat16)
    scores = lax.dot_general(queries, targets, (((1,), (1,)), ((), ())), preferred_element_type=jnp.float32)
    slot_ids = jnp.arange(sources.shape[0], dtype=jnp.int32)
    is_live = slot_ids < live_count
    exp_terms = jnp.where(is_live[None, :], jnp.exp(scores), jnp.float32(0.0))
    probability = exp_terms / lax.optimization_barrier(jnp.sum(exp_terms, axis=1, keepdims=True))
    diagonal = (slot_ids[:, None] == slot_ids[None, :]).astype(jnp.float32)
    coeffs = jnp.where(is_live[:, None], probability - diagonal, jnp.float32(0.0)).astype(jnp.bfloat16)
    d_queries = jnp.dot(coeffs, targets, preferred_element_type=jnp.float32)
    d_keys = lax.dot_general(coeffs, queries, (((0,), (0,)), ((), ())), preferred_element_type=jnp.float32).astype(jnp.bfloat16)
    dq_re, dq_im = (d_queries[:, :half_width], d_queries[:, half_width:])
    d_src = jnp.concatenate([dq_re * rel_re + dq_im * rel_im, dq_im * rel_re - dq_re * rel_im], axis=1).astype(jnp.bfloat16)
    d_rel = jnp.concatenate([dq_re * src_re + dq_im * src_im, dq_im * src_re - dq_re * src_im], axis=1).astype(jnp.bfloat16)
    return (d_src, d_rel, d_keys)

def row_adagrad(table_rows, adagrad_state, gradients):
    new_state = adagrad_state + lax.optimization_barrier(jnp.mean(gradients * gradients, axis=1))
    return (table_rows - learning_rate * gradients / (jnp.sqrt(new_state)[:, None] + epsilon), new_state)

def reference(entity_table, entity_state, relation_table, relation_state, source_rows, target_rows, relation_ids, live_counts):
    table_now = entity_table
    state_now = entity_state
    relation_b = relation_table.astype(jnp.bfloat16)
    relation_total = jnp.zeros((RELS, W), jnp.float32)
    for round_idx in range(2):
        offset = 1 if round_idx == 0 else N_DOM // 2
        blocks = table_now.astype(jnp.bfloat16).reshape(N_DOM, ROWS_DEV, W)
        partner_blocks = jnp.roll(blocks, -offset, axis=0)
        src_all = source_rows[round_idx].reshape(N_DOM, N_REP, GROUP)
        tgt_all = target_rows[round_idx].reshape(N_DOM, N_REP, GROUP)
        kind_all = relation_ids[round_idx].reshape(N_DOM, N_REP, GROUP)
        count_all = live_counts[round_idx]

        def partition(items):
            own_block, partner_block, src_part, tgt_part, kind_part, count_part = items
            src_sum = jnp.zeros((ROWS_DEV, W), jnp.float32)
            tgt_sum = jnp.zeros((ROWS_DEV, W), jnp.float32)
            rel_sum = jnp.zeros((RELS, W), jnp.float32)
            for rep_index in range(N_REP):
                source_b = lookup(src_part[rep_index], own_block)
                relation_rows = lookup(kind_part[rep_index], relation_b)
                target_b = lookup(tgt_part[rep_index], partner_block)
                d_src, d_rel, d_keys = group_terms(source_b, relation_rows, target_b, count_part[rep_index])
                src_sum = src_sum + spread_rows(src_part[rep_index], ROWS_DEV, d_src)
                tgt_sum = tgt_sum + spread_rows(tgt_part[rep_index], ROWS_DEV, d_keys)
                rel_sum = rel_sum + spread_rows(kind_part[rep_index], RELS, d_rel)
            return (src_sum, tgt_sum, rel_sum)
        src_grads, tgt_grads, rel_grads = lax.map(partition, (blocks, partner_blocks, src_all, tgt_all, kind_all, count_all))
        table_grads = src_grads + jnp.roll(tgt_grads, offset, axis=0)
        table_now, state_now = row_adagrad(table_now, state_now, table_grads.reshape(ENTITIES, W))
        relation_total = relation_total + lax.optimization_barrier(jnp.sum(rel_grads, axis=0))
    new_relations, new_relation_state = row_adagrad(relation_table, relation_state, relation_total)
    return (table_now, state_now, new_relations, new_relation_state)
```

```python
import functools

import jax
import jax.numpy as jnp
from jax import lax
from jax.experimental import pallas as pl
from jax.experimental.pallas import tpu as pltpu
from jax.sharding import PartitionSpec as P

MESH = pl.DeviceIdType.MESH
F32, BF16, I32 = jnp.float32, jnp.bfloat16, jnp.int32

RATE = 0.2
EPS = 1e-06
W = 400
HALF = 200
WIDE = 512
ROWS = 4096
SHARE = 1024
GROUP = 256
RELS = 1300
SLOTS = 1536
FIRST = 1024
CHUNKS = 2

SRC, TGT, RID = 0, 2, 4


def mat(a, b):
    return jnp.dot(a, b, preferred_element_type=F32)


def iota(shape, dim):
    return lax.broadcasted_iota(I32, shape, dim)


def to_column(row):
    eye = iota((128, 128), 0) == iota((128, 128), 1)
    parts = [
        jnp.sum(jnp.where(eye, row[:, k : k + 128], jnp.zeros((), row.dtype)), axis=1, keepdims=True)
        for k in range(0, row.shape[1], 128)
    ]
    return jnp.concatenate(parts, axis=0)


def to_row(column):
    eye = iota((128, 128), 0) == iota((128, 128), 1)
    return jnp.sum(jnp.where(eye, column, 0.0), axis=0, keepdims=True)


def block_terms(src, rel, tgt, live):
    s_re, s_im = src[:, :HALF], src[:, HALF:]
    r_re, r_im = rel[:, :HALF], rel[:, HALF:]
    queries = jnp.concatenate([s_re * r_re - s_im * r_im, s_re * r_im + s_im * r_re], axis=1).astype(BF16)
    scores = lax.dot_general(queries, tgt, (((1,), (1,)), ((), ())), preferred_element_type=F32)
    row_id, col_id = iota((GROUP, GROUP), 0), iota((GROUP, GROUP), 1)
    terms = jnp.where(col_id < live, jnp.exp(scores), 0.0)
    probs = terms / jnp.sum(terms, axis=1, keepdims=True)
    coeffs = jnp.where(row_id < live, probs - jnp.where(row_id == col_id, 1.0, 0.0), 0.0)
    coeffs_b = coeffs.astype(BF16)
    d_queries = mat(coeffs_b, tgt)
    d_keys = mat(coeffs.T.astype(BF16), queries).astype(BF16)
    q_re, q_im = d_queries[:, :HALF], d_queries[:, HALF:]
    d_rel = jnp.concatenate([q_re * s_re + q_im * s_im, q_im * s_re - q_re * s_im], axis=1).astype(BF16)
    d_src = jnp.concatenate([q_re * r_re + q_im * r_im, q_im * r_re - q_re * r_im], axis=1).astype(BF16)
    return d_src, d_rel, d_keys


def adagrad(rows, state, grads):
    state = state + jnp.sum(grads * grads, axis=1, keepdims=True) * (1.0 / W)
    return rows - RATE * grads / (jnp.sqrt(state) + EPS), state


def summed(ids, slot_ids, values):
    return mat(jnp.where(ids == slot_ids, 1.0, 0.0).astype(BF16), values)


def kernel(
    tab_hbm, rtab_hbm, state_v, state_s, rstate_s, idx_s, idx_v, live_s,
    ent_hbm, est_ref, rel_hbm, rmean_ref,
    tab, rtab, idx_in, req_s, comb, slot0, slot1,
    rows_a, rows_b, src1, req1, st_src1, st_req1, rel0, rel1,
    out_rows, tgt_in, back, c0, c1, own, own_st,
    drel, hsum, hsend, cin, xin, qsum, qsend, zin, yin, rst, dall,
    local_sem, send_sem, recv_sem,
):
    dom, rep = lax.axis_index("dom"), lax.axis_index("rep")
    core, y_lo = lax.rem(rep, 2), lax.div(rep, 2)
    x, z, y_hi = lax.rem(dom, 4), lax.rem(lax.div(dom, 4), 8), lax.div(dom, 32)
    y = 2 * y_hi + y_lo
    plane = 32 * y_hi

    core_mate = (dom, rep + 1 - 2 * core)
    y_mate = (dom, lax.rem(rep + 2, 4))
    cross_mate = (dom, lax.rem(rep + 2, 4) + 1 - 2 * core)
    after = (lax.rem(dom + 1, 64), rep)
    before = (lax.rem(dom + 63, 64), rep)
    other = (lax.rem(dom + 32, 64), lax.rem(rep + 2, 4))
    opposite = (lax.rem(dom + 32, 64), rep)
    x_peers = [(plane + 4 * z + lax.rem(x + k, 4), rep) for k in range(1, 4)]
    z_peers = [(plane + 4 * lax.rem(z + k, 8) + x, rep) for k in range(1, 8)]

    count = [0]

    def send(src, dst, device):
        i = count[0]
        count[0] += 1
        return pltpu.make_async_remote_copy(
            src_ref=src, dst_ref=dst, send_sem=send_sem.at[i], recv_sem=recv_sem.at[i],
            device_id=device, device_id_type=MESH,
        )

    def start(copies):
        for copy in copies:
            copy.start()

    load_tab = pltpu.make_async_copy(tab_hbm, tab, local_sem.at[0])
    load_rtab = pltpu.make_async_copy(rtab_hbm, rtab, local_sem.at[1])
    load_tab.start()
    load_rtab.start()

    barrier = pltpu.get_barrier_semaphore()
    greeted = [core_mate, y_mate, cross_mate, after, before, other, opposite] + x_peers + z_peers
    for device in greeted:
        pl.semaphore_signal(barrier, inc=1, device_id=device, device_id_type=MESH)
    pl.semaphore_wait(barrier, len(greeted))

    ask0 = send(idx_v, idx_in.at[0], after)
    ask1 = send(idx_v, idx_in.at[1], other)
    start([ask0, ask1])

    def gather(dst, table, index_of, state=None):
        def eight(g, carry):
            base = pl.multiple_of(g * 8, 8)
            for k in range(8):
                i = index_of(base + k)
                dst[pl.ds(base + k, 1), :] = table[pl.ds(i, 1), :]
                if state is not None:
                    state[pl.ds(base + k, 1), :] = jnp.full((1, 128), state_s[i], F32)
            return carry

        lax.fori_loop(0, GROUP // 8, eight, 0)

    load_rtab.wait()
    gather(rel0, rtab, lambda j: idx_s[RID, j])
    ask0.wait_recv()
    fetch0 = pltpu.make_async_copy(idx_in.at[0], req_s.at[0], local_sem.at[2])
    fetch0.start()
    load_tab.wait()
    fetch0.wait()
    gather(rows_a, tab, lambda j: req_s[0, TGT, j])
    out_rows[0] = rows_a[...].astype(BF16)
    rows_out0 = send(out_rows.at[0], tgt_in.at[0], before)
    rows_out0.start()

    gather(rows_b, tab, lambda j: idx_s[SRC, j])
    ask1.wait_recv()
    fetch1 = pltpu.make_async_copy(idx_in.at[1], req_s.at[1], local_sem.at[3])
    fetch1.start()
    comb[rep, 0:2, :] = idx_v[SRC : SRC + 2, :]
    comb[rep, 2:3, :] = idx_in[0, TGT : TGT + 1, :]
    comb[rep, 3:4, :] = idx_in[1, TGT + 1 : TGT + 2, :]
    comb[rep, 4:8, :] = jnp.zeros((4, GROUP), I32)
    combs = [send(comb.at[rep], comb.at[rep], device) for device in (core_mate, y_mate, cross_mate)]
    start(combs)
    fetch1.wait()
    gather(src1, tab, lambda j: idx_s[SRC + 1, j], st_src1)
    gather(req1, tab, lambda j: req_s[1, TGT + 1, j], st_req1)
    gather(rel1, rtab, lambda j: idx_s[RID + 1, j])

    first_rel = jnp.where(core == 0, (x * 8 + z) * 32, FIRST + (z * 4 + x) * 16)
    for k in range(32):
        rst[k : k + 1, :] = jnp.full((1, 128), rstate_s[jnp.minimum(first_rel + k, RELS - 1)], F32)

    drel[...] = jnp.zeros(drel.shape, BF16)
    own_rows = pl.multiple_of(rep * SHARE, SHARE)
    for k in range(8):
        own_st[k * 128 : (k + 1) * 128, :] = to_column(state_v[pl.ds(rep * 8 + k, 1), :])

    def block_at(ref, holder, kind, piece):
        size = GROUP // CHUNKS
        return ref.at[pl.ds(pl.multiple_of((2 * holder + kind) * GROUP + piece * size, size), size), :]

    def share_in_rep(ref, kind, piece):
        mine = block_at(ref, rep, kind, piece)
        to_core, to_y = send(mine, mine, core_mate), send(mine, mine, y_mate)
        got = block_at(ref, lax.rem(rep + 2, 4), kind, piece)
        onward = send(got, got, core_mate)
        return to_core, to_y, onward

    def round_terms(t, src, rel, c_ref, to):
        d_src, d_rel, d_keys = block_terms(src, rel, tgt_in[t], live_s[t, 0])
        back[t] = d_keys
        drel[t * GROUP : (t + 1) * GROUP, 0:W] = d_rel
        c_ref[pl.ds(pl.multiple_of((2 * rep) * GROUP, GROUP), GROUP), :] = d_src
        size = GROUP // CHUNKS
        return [
            send(back.at[t, pl.ds(k * size, size), :], block_at(c_ref, to[1], 1, k), to) for k in range(CHUNKS)
        ]

    src0_f = rows_b[...].astype(BF16).astype(F32)
    rel0_f = rel0[...].astype(BF16).astype(F32)
    rows_out0.wait_recv()
    backs0 = round_terms(0, src0_f, rel0_f, c0, after)
    shares0 = [share_in_rep(c0, 0, k) for k in range(CHUNKS)] + [share_in_rep(c0, 1, k) for k in range(CHUNKS)]
    start(backs0)
    for k in range(CHUNKS):
        start(shares0[k][:2])
    for copy in combs:
        copy.wait_recv()
    for b in range(4):
        for kind in range(2):
            at = (2 * b + kind) * GROUP
            slot0[0:1, at : at + GROUP] = comb[b, 2 * kind : 2 * kind + 1, :]
            slot1[0:1, at : at + GROUP] = comb[b, 2 * kind + 1 : 2 * kind + 2, :]
    src1_ids = to_column(idx_v[SRC + 1 : SRC + 2, :])
    req1_ids = to_column(idx_in[1, TGT + 1 : TGT + 2, :])
    for k in range(CHUNKS):
        backs0[k].wait_recv()
        start(shares0[CHUNKS + k][:2])
        shares0[k][1].wait_recv()
        shares0[k][2].start()
    for k in range(CHUNKS):
        shares0[CHUNKS + k][1].wait_recv()
        shares0[CHUNKS + k][2].start()
    for group in shares0:
        group[0].wait_recv()
        group[2].wait_recv()

    def updated(rows, state, ids):
        grads = summed(ids, slot0[0:1, :], c0[...])
        return adagrad(rows[...], state[:, 0:1], grads)[0].astype(BF16)

    out_rows[1] = updated(req1, st_req1, req1_ids)
    rows_out1 = send(out_rows.at[1], tgt_in.at[1], other)
    rows_out1.start()
    src1_f = updated(src1, st_src1, src1_ids).astype(F32)
    rel1_f = rel1[...].astype(BF16).astype(F32)

    def relation_part(tile, t):
        ids = iota((GROUP, 1), 0) + tile * GROUP
        return summed(ids, idx_v[RID + t : RID + t + 1, :], drel[t * GROUP : (t + 1) * GROUP, :])

    for tile in range(SLOTS // GROUP):
        hsum[tile * GROUP : (tile + 1) * GROUP, :] = relation_part(tile, 0)

    def own_step(tile, rows, slots, c_ref):
        lo = tile * GROUP
        ids = iota((GROUP, 1), 0) + (rep * SHARE + lo)
        grads = summed(ids, slots[0:1, :], c_ref[...])
        new_rows, new_state = adagrad(rows, own_st[lo : lo + GROUP, :], grads)
        own[lo : lo + GROUP, :] = new_rows
        own_st[lo : lo + GROUP, :] = new_state

    for tile in range(SHARE // GROUP):
        own_step(tile, tab[pl.ds(own_rows + tile * GROUP, GROUP), :], slot0, c0)

    rows_out1.wait_recv()
    backs1 = round_terms(1, src1_f, rel1_f, c1, other)
    shares1 = [share_in_rep(c1, 0, k) for k in range(CHUNKS)] + [share_in_rep(c1, 1, k) for k in range(CHUNKS)]
    for tile in range(SLOTS // GROUP):
        rows = slice(tile * GROUP, (tile + 1) * GROUP)
        both = hsum[rows, :] + relation_part(tile, 1)
        hsum[rows, :] = both
        hsend[rows, :] = both.astype(BF16)

    on_0, on_1 = core == 0, core == 1

    def at(ref, lo, size):
        return ref.at[pl.ds(pl.multiple_of(lo, size), size), :]

    def f32_at(ref, lo, size):
        return ref[pl.ds(pl.multiple_of(lo, size), size), :].astype(F32)

    core_0 = send(hsend.at[pl.ds(FIRST, SLOTS - FIRST), :], cin.at[pl.ds(0, SLOTS - FIRST), :], core_mate)
    core_1 = send(hsend.at[pl.ds(0, FIRST), :], cin, core_mate)

    @pl.when(on_0)
    def _():
        core_0.start()

    @pl.when(on_1)
    def _():
        core_1.start()

    start(backs1)
    for k in range(CHUNKS):
        start(shares1[k][:2])

    wide_x = [
        send(at(hsend, lax.rem(x + k, 4) * 256, 256), xin.at[pl.ds((k - 1) * 256, 256), :], x_peers[k - 1])
        for k in range(1, 4)
    ]
    wide_z = [
        send(at(hsend, FIRST + lax.rem(z + k, 8) * 64, 64), xin.at[pl.ds((k - 1) * 64, 64), :], z_peers[k - 1])
        for k in range(1, 8)
    ]
    thin_z = [
        send(at(qsend, lax.rem(z + k, 8) * 32, 32), zin.at[pl.ds((k - 1) * 32, 32), :], z_peers[k - 1])
        for k in range(1, 8)
    ]
    thin_x = [
        send(at(qsend, lax.rem(x + k, 4) * 16, 16), zin.at[pl.ds((k - 1) * 16, 16), :], x_peers[k - 1])
        for k in range(1, 4)
    ]

    def spread(first, place, parts, size, copies):
        for k in range(1, parts):
            lo = lax.rem(place + k, parts) * size
            hsend[pl.ds(pl.multiple_of(first + lo, size), size), :] = (
                f32_at(hsum, first + lo, size) + f32_at(cin, lo, size)
            ).astype(BF16)
            copies[k - 1].start()
        lo = place * size
        qsum[0:size, :] = f32_at(hsum, first + lo, size) + f32_at(cin, lo, size)

    def collect(parts, size, copies, landing):
        total = qsum[0:size, :]
        for k in range(1, parts):
            copies[k - 1].wait_recv()
            total = total + landing[(k - 1) * size : k * size, :].astype(F32)
        return total

    @pl.when(on_0)
    def _():
        core_1.wait_recv()
        core_0.wait_send()
        spread(0, x, 4, 256, wide_x)

    @pl.when(on_1)
    def _():
        core_0.wait_recv()
        core_1.wait_send()
        spread(FIRST, z, 8, 64, wide_z)

    for k in range(CHUNKS):
        backs1[k].wait_recv()
        start(shares1[CHUNKS + k][:2])
        shares1[k][1].wait_recv()
        shares1[k][2].start()

    @pl.when(on_0)
    def _():
        total = collect(4, 256, wide_x, xin)
        qsum[...] = total
        qsend[...] = total.astype(BF16)
        start(thin_z)

    @pl.when(on_1)
    def _():
        total = collect(8, 64, wide_z, xin)
        qsum[0:64, :] = total
        qsend[0:64, :] = total.astype(BF16)
        start(thin_x)

    for k in range(CHUNKS):
        shares1[CHUNKS + k][1].wait_recv()
        shares1[CHUNKS + k][2].start()

    def last(place, parts, size, copies):
        total = f32_at(qsum, place * size, size)
        for k in range(1, parts):
            copies[k - 1].wait_recv()
            total = total + zin[(k - 1) * size : k * size, :].astype(F32)
        yin[y, 0:size, :] = total.astype(BF16)

    @pl.when(on_0)
    def _():
        last(z, 8, 32, thin_z)

    @pl.when(on_1)
    def _():
        last(x, 4, 16, thin_x)
        yin[y, 16:32, :] = jnp.zeros((16, WIDE), BF16)

    y_sends = [send(yin.at[y], yin.at[y], device) for device in (y_mate, opposite, other)]
    start(y_sends)
    for copy in y_sends:
        copy.wait_recv()

    total = yin[0].astype(F32) + yin[1].astype(F32) + yin[2].astype(F32) + yin[3].astype(F32)
    mean = jnp.sum(total * total, axis=1, keepdims=True) * (1.0 / W)
    delta = -RATE * total / (jnp.sqrt(rst[:, 0:1] + mean) + EPS)
    mean_hi = mean.astype(BF16).astype(F32)
    lane = iota((32, WIDE), 1)
    delta = jnp.where(lane == W, mean_hi, jnp.where(lane == W + 1, mean - mean_hi, delta)).astype(BF16)

    x_row, z_row = x * 256, FIRST + z * 64
    own_0 = at(dall, x_row + z * 32, 32)
    own_1 = at(dall, z_row + x * 16, 16)
    out_z = [send(own_0, own_0, device) for device in z_peers]
    out_x = [send(own_1, own_1, device) for device in x_peers]
    all_0, all_1 = at(dall, x_row, 256), at(dall, z_row, 64)
    out_x2 = [send(all_0, all_0, device) for device in x_peers]
    out_z2 = [send(all_1, all_1, device) for device in z_peers]
    half_0, half_1 = dall.at[pl.ds(0, FIRST), :], dall.at[pl.ds(FIRST, SLOTS - FIRST), :]
    swap_0, swap_1 = send(half_0, half_0, core_mate), send(half_1, half_1, core_mate)

    @pl.when(on_0)
    def _():
        own_0[...] = delta
        start(out_z)

    @pl.when(on_1)
    def _():
        own_1[...] = delta[0:16, :]
        start(out_x)

    for group in shares1:
        group[0].wait_recv()
        group[2].wait_recv()

    def own_tiles(tiles):
        for tile in tiles:
            lo = tile * GROUP
            own_step(tile, own[lo : lo + GROUP, :], slot1, c1)

    own_tiles((0, 1))

    @pl.when(on_0)
    def _():
        for copy in out_z:
            copy.wait_recv()
        start(out_x2)

    @pl.when(on_1)
    def _():
        for copy in out_x:
            copy.wait_recv()
        start(out_z2)

    own_tiles((2, 3))
    store_own = pltpu.make_async_copy(own, ent_hbm, local_sem.at[4])
    store_own.start()
    for k in range(8):
        est_ref[k : k + 1, :] = to_row(own_st[k * 128 : (k + 1) * 128, :])

    @pl.when(on_0)
    def _():
        for copy in out_x2:
            copy.wait_recv()
        swap_0.start()
        swap_1.wait_recv()

    @pl.when(on_1)
    def _():
        for copy in out_z2:
            copy.wait_recv()
        swap_1.start()
        swap_0.wait_recv()

    rtab[...] = rtab[...] + dall[0:RELS, 0:W].astype(F32)
    store_rel = pltpu.make_async_copy(rtab, rel_hbm, local_sem.at[5])
    store_rel.start()
    for k in range(SLOTS // 128):
        part = dall[k * 128 : (k + 1) * 128, 384:512].astype(F32)
        rmean_ref[k : k + 1, :] = to_row(part[:, 16:17] + part[:, 17:18])

    for copy in [ask0, ask1, rows_out0, rows_out1] + combs + backs0 + backs1 + y_sends:
        copy.wait_send()
    for group in shares0 + shares1:
        for copy in group:
            copy.wait_send()

    @pl.when(on_0)
    def _():
        for copy in wide_x + thin_z + out_z + out_x2 + [swap_0]:
            copy.wait_send()

    @pl.when(on_1)
    def _():
        for copy in wide_z + thin_x + out_x + out_z2 + [swap_1]:
            copy.wait_send()

    store_own.wait()
    store_rel.wait()
    assert count[0] <= SEMS, count[0]


SEMS = 96


def per_device(
    entity_table, entity_state, relation_table, relation_state, source_rows, target_rows, relation_ids, live_counts
):
    idx = jnp.concatenate(
        [source_rows[:, 0], target_rows[:, 0], relation_ids[:, 0], jnp.zeros((2, GROUP), I32)], axis=0
    )
    vmem, smem = pl.BlockSpec(memory_space=pltpu.VMEM), pl.BlockSpec(memory_space=pltpu.SMEM)
    anywhere = pl.BlockSpec(memory_space=pl.ANY)
    block_f = pltpu.VMEM((GROUP, W), F32)
    splat = pltpu.VMEM((GROUP, 128), F32)
    blocks_b = pltpu.VMEM((2, GROUP, W), BF16)
    contributions = pltpu.VMEM((8 * GROUP, W), BF16)
    own, own_state, new_relations, mean = pl.pallas_call(
        kernel,
        out_shape=(
            jax.ShapeDtypeStruct((SHARE, W), F32),
            jax.ShapeDtypeStruct((8, 128), F32),
            jax.ShapeDtypeStruct((RELS, W), F32),
            jax.ShapeDtypeStruct((SLOTS // 128, 128), F32),
        ),
        in_specs=[anywhere, anywhere, vmem, smem, smem, smem, vmem, smem],
        out_specs=(anywhere, vmem, anywhere, vmem),
        scratch_shapes=[
            pltpu.VMEM((ROWS, W), F32),
            pltpu.VMEM((RELS, W), F32),
            pltpu.VMEM((2, 8, GROUP), I32),
            pltpu.SMEM((2, 8, GROUP), I32),
            pltpu.VMEM((4, 8, GROUP), I32),
            pltpu.VMEM((8, 8 * GROUP), I32),
            pltpu.VMEM((8, 8 * GROUP), I32),
            block_f, block_f, block_f, block_f,
            splat, splat,
            block_f, block_f,
            blocks_b, blocks_b, blocks_b,
            contributions, contributions,
            pltpu.VMEM((SHARE, W), F32),
            pltpu.VMEM((SHARE, 1), F32),
            pltpu.VMEM((2 * GROUP, WIDE), BF16),
            pltpu.VMEM((SLOTS, WIDE), F32),
            pltpu.VMEM((SLOTS, WIDE), BF16),
            pltpu.VMEM((FIRST, WIDE), BF16),
            pltpu.VMEM((768, WIDE), BF16),
            pltpu.VMEM((256, WIDE), F32),
            pltpu.VMEM((256, WIDE), BF16),
            pltpu.VMEM((224, WIDE), BF16),
            pltpu.VMEM((4, 32, WIDE), BF16),
            pltpu.VMEM((32, 128), F32),
            pltpu.VMEM((SLOTS, WIDE), BF16),
            pltpu.SemaphoreType.DMA((6,)),
            pltpu.SemaphoreType.DMA((SEMS,)),
            pltpu.SemaphoreType.DMA((SEMS,)),
        ],
        compiler_params=pltpu.CompilerParams(
            collective_id=0, has_side_effects=True, vmem_limit_bytes=56 * 1024 * 1024
        ),
    )(
        entity_table, relation_table, entity_state.reshape(ROWS // 128, 128), entity_state, relation_state, idx, idx,
        live_counts[:, 0],
    )
    new_state = relation_state + mean.reshape(-1)[:RELS]
    return own, own_state.reshape(-1), new_relations, new_state


def solution(mesh):
    in_specs = (
        P("dom", None),
        P("dom"),
        P(),
        P(),
        P(None, "dom", "rep"),
        P(None, "dom", "rep"),
        P(None, "dom", "rep"),
        P(None, "dom", "rep"),
    )
    out_specs = (P(("dom", "rep"), None), P(("dom", "rep")), P(), P())
    return jax.shard_map(per_device, mesh=mesh, in_specs=in_specs, out_specs=out_specs, check_vma=False)
```

```python
import jax
import jax.numpy as jnp
from jax import lax
from jax.experimental import pallas as pl
from jax.experimental.pallas import tpu as pltpu
from jax.sharding import PartitionSpec as P

MESH = pl.DeviceIdType.MESH
F32, BF16, I32 = jnp.float32, jnp.bfloat16, jnp.int32

RATE = 0.2
EPS = 1e-06
W = 400
HALF = 200
TALL = 416
WIDE = 512
ROWS = 4096
SHARE = 1024
GROUP = 256
RELS = 1300
FIRST = 1024
SECOND = 384
SLOTS = FIRST + SECOND
PER_0, PER_1 = 32, 48
PIECES = ((0, 208), (208, 192))
SEMS = 112


def mat(a, b):
    return jnp.dot(a, b, preferred_element_type=F32)


def iota(shape, dim):
    return lax.broadcasted_iota(I32, shape, dim)


def indicator(hit):
    return jnp.where(hit, 1.0, 0.0).astype(BF16)


def columns(rows):
    eye = indicator(iota((GROUP, GROUP), 0) == iota((GROUP, GROUP), 1))

    def turned(part):
        return lax.dot_general(
            eye, part.astype(F32).astype(BF16), (((1,), (1,)), ((), ())), preferred_element_type=F32
        )

    return turned(lax.shift_right_logical(rows, 8)) * 256.0 + turned(jnp.bitwise_and(rows, 255))


def adagrad(rows, state, grads):
    state = state + jnp.sum(grads * grads, axis=0, keepdims=True) * (1.0 / W)
    return rows - RATE * grads / (jnp.sqrt(state) + EPS), state


def kernel(
    tab_hbm, rtab_hbm, state_v, rstate_s, src_v, tgt_v, rid_v, live_s,
    ent_hbm, est_ref, rel_hbm, rmean_ref,
    tab, rtab, parts, rtab_b, st_parts, msg, idx_in, comb, cid,
    out_rows, tgt_in, back, c0, c1, gsum, own, own_st,
    h0, hsend, cin0, cin1, xin, qsum, hrow, zin, xex, yin, rst, drow, dout, dall,
    local_sem, send_sem, recv_sem,
):
    dom, rep = lax.axis_index("dom"), lax.axis_index("rep")
    core, y_lo = lax.rem(rep, 2), lax.div(rep, 2)
    x, z, y_hi = lax.rem(dom, 4), lax.rem(lax.div(dom, 4), 8), lax.div(dom, 32)
    y = 2 * y_hi + y_lo
    plane = 32 * y_hi
    on_0, on_1 = core == 0, core == 1

    core_rep, y_rep = rep + 1 - 2 * core, lax.rem(rep + 2, 4)
    core_mate, y_mate = (dom, core_rep), (dom, y_rep)
    cross_mate = (dom, y_rep + 1 - 2 * core)
    after = (lax.rem(dom + 1, 64), rep)
    before = (lax.rem(dom + 63, 64), rep)
    other = (lax.rem(dom + 32, 64), y_rep)
    opposite = (lax.rem(dom + 32, 64), rep)
    x_peers = [(plane + 4 * z + lax.rem(x + k, 4), rep) for k in range(1, 4)]
    z_peers = [(plane + 4 * lax.rem(z + k, 8) + x, rep) for k in range(1, 8)]

    count = [0]

    def send(src, dst, device):
        i = count[0]
        count[0] += 1
        assert i < SEMS
        return pltpu.make_async_remote_copy(
            src_ref=src, dst_ref=dst, send_sem=send_sem.at[i], recv_sem=recv_sem.at[i],
            device_id=device, device_id_type=MESH,
        )

    def start(copies):
        for copy in copies:
            copy.start()

    def lanes(ref, lo, size):
        return ref.at[:, pl.ds(pl.multiple_of(lo, 128), size)]

    def at_rows(ref, lo, size):
        return ref.at[pl.ds(pl.multiple_of(lo, 16), size), :]

    loads = [
        pltpu.make_async_copy(lanes(tab_hbm, k * 1024, 1024), lanes(tab, k * 1024, 1024), local_sem.at[k])
        for k in range(4)
    ]
    start(loads)
    load_rtab = pltpu.make_async_copy(rtab_hbm, rtab, local_sem.at[4])
    load_rtab.start()

    barrier = pltpu.get_barrier_semaphore()
    greeted = [core_mate, y_mate, cross_mate, after, before, other, opposite] + x_peers + z_peers
    for device in greeted:
        pl.semaphore_signal(barrier, inc=1, device_id=device, device_id_type=MESH)
    for t in range(2):
        msg[t : t + 1, :] = src_v[t]
        msg[2 + t : 3 + t, :] = tgt_v[t]
        msg[4 + t : 5 + t, :] = rid_v[t]
    msg[6:8, :] = jnp.zeros((2, GROUP), I32)
    pl.semaphore_wait(barrier, len(greeted))

    ask0 = send(msg, idx_in.at[0], after)
    ask1 = send(msg, idx_in.at[1], other)
    start([ask0, ask1])

    def lookup(table, ids):
        return mat(table, indicator(iota((table.shape[1], GROUP), 0) == ids))

    def high(k, carry):
        at = pl.ds(pl.multiple_of(k * 256, 256), 256)
        parts[0:W, at] = tab[:, at].astype(BF16)
        return carry

    for k in range(4):
        loads[k].wait()
        lax.fori_loop(4 * k, 4 * k + 4, high, 0)

    ask0.wait_recv()
    out_rows[0] = lookup(parts[0:W, :], idx_in[0, 2:3, :]).astype(BF16)
    rows_out0 = send(out_rows.at[0], tgt_in.at[0], before)
    rows_out0.start()
    ask1.wait_recv()

    comb[rep, 0:2, :] = msg[0:2, :]
    comb[rep, 2:3, :] = idx_in[0, 2:3, :]
    comb[rep, 3:4, :] = idx_in[1, 3:4, :]
    comb[rep, 4:8, :] = jnp.zeros((4, GROUP), I32)
    combs = [send(comb.at[rep], comb.at[rep], device) for device in (core_mate, y_mate, cross_mate)]
    start(combs)

    def product(a, b):
        return jnp.concatenate(
            [a[:HALF] * b[:HALF] - a[HALF:] * b[HALF:], a[:HALF] * b[HALF:] + a[HALF:] * b[:HALF]], axis=0
        )

    def conj_product(a, b):
        return jnp.concatenate(
            [a[:HALF] * b[:HALF] + a[HALF:] * b[HALF:], a[HALF:] * b[:HALF] - a[:HALF] * b[HALF:]], axis=0
        )

    def coefficients(queries_row, tgt, live):
        scores = mat(queries_row, tgt)
        row_id, col_id = iota((GROUP, GROUP), 0), iota((GROUP, GROUP), 1)
        terms = jnp.where(col_id < live, jnp.exp(scores), 0.0)
        probs = terms / jnp.sum(terms, axis=1, keepdims=True)
        return jnp.where(row_id < live, probs - jnp.where(row_id == col_id, 1.0, 0.0), 0.0)

    src0 = lookup(parts[0:W, :], msg[0:1, :])
    load_rtab.wait()
    rtab_b[...] = rtab[...].astype(BF16)
    rel0 = lookup(rtab_b[...], msg[4:5, :])
    queries0 = product(src0, rel0)
    queries0_row = queries0.T.astype(BF16)
    queries0 = queries0.astype(BF16)

    def low(k, carry):
        at = pl.ds(pl.multiple_of(k * 256, 256), 256)
        parts[W : 2 * W, at] = (tab[:, at] - parts[0:W, at].astype(F32)).astype(BF16)
        return carry

    lax.fori_loop(0, ROWS // 256, low, 0)
    st_parts[...] = jnp.zeros(st_parts.shape, F32)
    for k in range(ROWS // 128):
        whole = state_v[k : k + 1, :]
        top = whole.astype(BF16).astype(F32)
        mid = (whole - top).astype(BF16).astype(F32)
        st_parts[0:1, k * 128 : (k + 1) * 128] = top
        st_parts[1:2, k * 128 : (k + 1) * 128] = mid
        st_parts[2:3, k * 128 : (k + 1) * 128] = whole - top - mid
    parts[2 * W : 2 * W + 16, :] = st_parts[...].astype(BF16)

    def lookup_f32(ids):
        got = lookup(parts[...], ids)
        state = got[2 * W : 2 * W + 1] + got[2 * W + 1 : 2 * W + 2] + got[2 * W + 2 : 2 * W + 3]
        return got[0:W] + got[W : 2 * W], state

    req1_ids, src1_ids = idx_in[1, 3:4, :], msg[1:2, :]
    req1, req1_st = lookup_f32(req1_ids)
    src1, src1_st = lookup_f32(src1_ids)
    rel1 = lookup(rtab_b[...], msg[5:6, :])
    own_ids = columns(msg[...])
    for copy in combs:
        copy.wait_recv()
    for b in range(4):
        turned = columns(comb[b])
        for q in range(4):
            cid[q, b * GROUP : (b + 1) * GROUP, :] = turned[:, q : q + 1]

    first_rel = jnp.where(on_0, (x * 8 + z) * PER_0, FIRST + z * PER_1)
    for k in range(PER_1):
        rst[k : k + 1, :] = jnp.full((1, 128), rstate_s[jnp.minimum(first_rel + k, RELS - 1)], F32)
    hrow[...] = jnp.zeros(hrow.shape, F32)
    for k in range(8):
        own_st[0:1, k * 128 : (k + 1) * 128] = state_v[pl.ds(rep * 8 + k, 1), :]

    def block_at(ref, holder, kind, piece):
        lo, size = PIECES[piece]
        return ref.at[pl.ds(lo, size), pl.ds(pl.multiple_of(kind * 1024 + holder * GROUP, GROUP), GROUP)]

    def share_in_rep(ref, kind, piece):
        mine, got = block_at(ref, rep, kind, piece), block_at(ref, y_rep, kind, piece)
        return send(mine, mine, core_mate), send(mine, mine, y_mate), send(got, got, core_mate)

    def back_copies(t, ref, to):
        return [
            send(back.at[t, pl.ds(lo, size), :], block_at(ref, to[1], 1, k), to)
            for k, (lo, size) in enumerate(PIECES)
        ]

    def share_copies(ref):
        return [[share_in_rep(ref, kind, k) for k in range(len(PIECES))] for kind in range(2)]

    def mine_at(ref):
        return pl.ds(pl.multiple_of(rep * GROUP, GROUP), GROUP)

    rows_out0.wait_recv()
    backs0, shares0 = back_copies(0, c0, after), share_copies(c0)
    coeffs = coefficients(queries0_row, tgt_in[0], live_s[0])
    back[0] = mat(queries0, coeffs.astype(BF16)).astype(BF16)
    start(backs0)
    d_queries = mat(tgt_in[0], coeffs.T.astype(BF16))
    c0[:, mine_at(c0)] = conj_product(d_queries, rel0).astype(BF16)
    for group in shares0[0]:
        start(group[:2])
    d_rel0 = conj_product(d_queries, src0).astype(BF16)

    def relation_part(d_rel, rid, lo, size):
        return mat(d_rel, indicator(rid == (iota((1, size), 1) + lo).astype(F32)))

    for lo in range(0, SLOTS, 128):
        h0[:, lo : lo + 128] = relation_part(d_rel0, own_ids[:, 4:5], lo, 128)

    for k in range(len(PIECES)):
        backs0[k].wait_recv()
        start(shares0[1][k][:2])
        shares0[0][k][1].wait_recv()
        shares0[0][k][2].start()
    for group in shares0[0]:
        group[0].wait_recv()
        group[2].wait_recv()

    def summed(ref, kind, q, ids):
        return mat(ref[:, kind * 1024 : (kind + 1) * 1024], indicator(cid[q] == ids.astype(F32)))

    own_first = rep * SHARE

    def tile_ids(tile):
        return iota((1, GROUP), 1) + (own_first + tile * GROUP)

    gsum[:, 0:256] = summed(c0, 0, 0, req1_ids)
    gsum[:, 256:512] = summed(c0, 0, 0, src1_ids)
    for group in shares0[1]:
        group[1].wait_recv()
        group[2].start()
    for group in shares0[1]:
        group[0].wait_recv()
        group[2].wait_recv()

    grads = gsum[:, 0:256] + summed(c0, 1, 2, req1_ids)
    out_rows[1] = adagrad(req1, req1_st, grads)[0].astype(BF16)
    rows_out1 = send(out_rows.at[1], tgt_in.at[1], other)
    rows_out1.start()
    grads = gsum[:, 256:512] + summed(c0, 1, 2, src1_ids)
    src1 = adagrad(src1, src1_st, grads)[0].astype(BF16).astype(F32)
    queries1 = product(src1, rel1)
    queries1_row = queries1.T.astype(BF16)
    queries1 = queries1.astype(BF16)

    for tile in range(SHARE // GROUP):
        at = slice(tile * GROUP, (tile + 1) * GROUP)
        grads = summed(c0, 0, 0, tile_ids(tile)) + summed(c0, 1, 2, tile_ids(tile))
        rows = tab[:, pl.ds(pl.multiple_of(own_first + tile * GROUP, GROUP), GROUP)]
        own[:, at], own_st[0:1, at] = adagrad(rows, own_st[0:1, at], grads)

    rows_out1.wait_recv()
    backs1, shares1 = back_copies(1, c1, other), share_copies(c1)
    coeffs = coefficients(queries1_row, tgt_in[1], live_s[1])
    d_queries = mat(tgt_in[1], coeffs.T.astype(BF16))
    d_rel1 = conj_product(d_queries, src1).astype(BF16)

    def relation_sum(lo, size):
        at = pl.ds(pl.multiple_of(lo, 128), size)
        return h0[:, at] + relation_part(d_rel1, own_ids[:, 5:6], lo, size)

    order = [lax.rem(x + k, 4) * 256 for k in (1, 2, 3, 0)]
    to_core_0 = [send(lanes(hsend, lo, 256), lanes(cin0, lo, 256), core_mate) for lo in order]
    to_core_1 = send(lanes(hsend, FIRST, SECOND), cin1, core_mate)
    wide_x = [send(lanes(hsend, order[k], 256), xin.at[k], x_peers[k]) for k in range(3)]
    wide_z = [
        send(at_rows(drow, lax.rem(z + k, 8) * PER_1, PER_1), zin.at[k - 1], z_peers[k - 1])
        for k in range(1, 8)
    ]
    thin_z = [
        send(at_rows(drow, lax.rem(z + k, 8) * PER_0, PER_0), zin.at[k - 1, pl.ds(0, PER_0), :], z_peers[k - 1])
        for k in range(1, 8)
    ]
    thin_x = [send(xex.at[x], xex.at[x], device) for device in x_peers]

    @pl.when(on_1)
    def _():
        for k in range(4):
            hsend[:, pl.ds(pl.multiple_of(order[k], 256), 256)] = relation_sum(order[k], 256).astype(BF16)
            to_core_0[k].start()

    @pl.when(on_0)
    def _():
        hsend[:, FIRST:SLOTS] = relation_sum(FIRST, SECOND).astype(BF16)
        to_core_1.start()

    back[1] = mat(queries1, coeffs.astype(BF16)).astype(BF16)
    start(backs1)
    c1[:, mine_at(c1)] = conj_product(d_queries, rel1).astype(BF16)
    for group in shares1[0]:
        start(group[:2])

    @pl.when(on_0)
    def _():
        for k in range(4):
            mine = relation_sum(order[k], 256)
            to_core_0[k].wait_recv()
            at = pl.ds(pl.multiple_of(order[k], 256), 256)
            mine = mine + cin0[:, at].astype(F32)
            if k < 3:
                hsend[:, at] = mine.astype(BF16)
                wide_x[k].start()
            else:
                qsum[:, 0:256] = mine

    @pl.when(on_1)
    def _():
        mine = relation_sum(FIRST, SECOND)
        to_core_1.wait_recv()
        turned = (mine + cin1[...].astype(F32)).T
        hrow[0:SECOND, 0:W] = turned
        drow[...] = hrow[...].astype(BF16)
        start(wide_z)

    for k in range(len(PIECES)):
        backs1[k].wait_recv()
        start(shares1[1][k][:2])
        shares1[0][k][1].wait_recv()
        shares1[0][k][2].start()

    def collect(copies, size, place):
        total = hrow[pl.ds(pl.multiple_of(place * size, 16), size), :]
        for k in range(7):
            copies[k].wait_recv()
            total = total + zin[k, 0:size, :].astype(F32)
        return total

    @pl.when(on_0)
    def _():
        total = qsum[:, 0:256]
        for k in range(3):
            wide_x[k].wait_recv()
            total = total + xin[k].astype(F32)
        hrow[0:256, 0:W] = total.T
        drow[0:256, :] = hrow[0:256, :].astype(BF16)
        start(thin_z)

    @pl.when(on_1)
    def _():
        xex[x] = collect(wide_z, PER_1, z).astype(BF16)
        start(thin_x)

    for group in shares1[1]:
        group[1].wait_recv()
        group[2].start()

    @pl.when(on_0)
    def _():
        yin[y, 0:PER_0, :] = collect(thin_z, PER_0, z).astype(BF16)
        yin[y, PER_0:PER_1, :] = jnp.zeros((PER_1 - PER_0, WIDE), BF16)

    @pl.when(on_1)
    def _():
        for copy in thin_x:
            copy.wait_recv()
        total = xex[0].astype(F32) + xex[1].astype(F32) + xex[2].astype(F32) + xex[3].astype(F32)
        yin[y] = total.astype(BF16)

    y_sends = [send(yin.at[y], yin.at[y], device) for device in (y_mate, opposite, other)]
    start(y_sends)
    for copy in y_sends:
        copy.wait_recv()

    total = yin[0].astype(F32) + yin[1].astype(F32) + yin[2].astype(F32) + yin[3].astype(F32)
    mean = jnp.sum(total * total, axis=1, keepdims=True) * (1.0 / W)
    delta = -RATE * total / (jnp.sqrt(rst[:, 0:1] + mean) + EPS)
    mean_hi = mean.astype(BF16).astype(F32)
    lane = iota((PER_1, WIDE), 1)
    delta = jnp.where(lane == W, mean_hi, jnp.where(lane == W + 1, mean - mean_hi, delta)).astype(BF16)

    own_0, own_1 = at_rows(dout, z * PER_0, PER_0), at_rows(dout, z * PER_1, PER_1)
    out_z0 = [send(own_0, own_0, device) for device in z_peers]
    out_z1 = [send(own_1, own_1, device) for device in z_peers]
    chunk = lanes(dall, x * 256, 256)
    out_x = [send(chunk, chunk, device) for device in x_peers]
    swap_0 = [send(chunk, chunk, core_mate)]
    for k in range(1, 4):
        got = lanes(dall, lax.rem(x + 4 - k, 4) * 256, 256)
        swap_0.append(send(got, got, core_mate))
    half_1 = lanes(dall, FIRST, SECOND)
    swap_1 = send(half_1, half_1, core_mate)

    @pl.when(on_0)
    def _():
        own_0[...] = delta[0:PER_0, :]
        start(out_z0)

    @pl.when(on_1)
    def _():
        own_1[...] = delta
        start(out_z1)

    for kind in range(2):
        for group in shares1[kind]:
            group[0].wait_recv()
            group[2].wait_recv()

    def own_tiles(tiles):
        for tile in tiles:
            at = slice(tile * GROUP, (tile + 1) * GROUP)
            grads = summed(c1, 0, 1, tile_ids(tile)) + summed(c1, 1, 3, tile_ids(tile))
            own[:, at], own_st[0:1, at] = adagrad(own[:, at], own_st[0:1, at], grads)

    own_tiles((0,))

    @pl.when(on_0)
    def _():
        for copy in out_z0:
            copy.wait_recv()
        dall[:, pl.ds(pl.multiple_of(x * 256, 256), 256)] = dout[0:256, :].astype(F32).T[0:TALL].astype(BF16)
        start(out_x)
        swap_0[0].start()

    @pl.when(on_1)
    def _():
        for copy in out_z1:
            copy.wait_recv()
        dall[:, FIRST:SLOTS] = dout[...].astype(F32).T[0:TALL].astype(BF16)
        swap_1.start()

    own_tiles((1, 2, 3))
    store_own = pltpu.make_async_copy(own, ent_hbm, local_sem.at[5])
    store_own.start()
    for k in range(8):
        est_ref[k : k + 1, :] = own_st[0:1, k * 128 : (k + 1) * 128]

    @pl.when(on_0)
    def _():
        for k in range(3):
            out_x[k].wait_recv()
            swap_0[k + 1].start()
        swap_1.wait_recv()

    @pl.when(on_1)
    def _():
        for copy in swap_0:
            copy.wait_recv()

    rtab[...] = rtab[...] + dall[0:W, 0:RELS].astype(F32)
    store_rel = pltpu.make_async_copy(rtab, rel_hbm, local_sem.at[6])
    store_rel.start()
    tail = dall[W:TALL, :].astype(F32)
    mean_row = tail[0:1, :] + tail[1:2, :]
    for k in range(SLOTS // 128):
        rmean_ref[k : k + 1, :] = mean_row[:, k * 128 : (k + 1) * 128]

    for copy in [ask0, ask1, rows_out0, rows_out1] + combs + backs0 + backs1 + y_sends:
        copy.wait_send()
    for group in shares0[0] + shares0[1] + shares1[0] + shares1[1]:
        for copy in group:
            copy.wait_send()

    @pl.when(on_0)
    def _():
        for copy in [to_core_1] + wide_x + thin_z + out_z0 + out_x + swap_0:
            copy.wait_send()

    @pl.when(on_1)
    def _():
        for copy in to_core_0 + wide_z + thin_x + out_z1 + [swap_1]:
            copy.wait_send()

    store_own.wait()
    store_rel.wait()


def per_device(
    entity_table, entity_state, relation_table, relation_state, source_rows, target_rows, relation_ids, live_counts
):
    vmem, smem = pl.BlockSpec(memory_space=pltpu.VMEM), pl.BlockSpec(memory_space=pltpu.SMEM)
    anywhere = pl.BlockSpec(memory_space=pl.ANY)
    contributions = pltpu.VMEM((W, 8 * GROUP), BF16)
    blocks = pltpu.VMEM((2, W, GROUP), BF16)
    own, own_state, new_relations, mean = pl.pallas_call(
        kernel,
        out_shape=(
            jax.ShapeDtypeStruct((W, SHARE), F32),
            jax.ShapeDtypeStruct((8, 128), F32),
            jax.ShapeDtypeStruct((W, RELS), F32),
            jax.ShapeDtypeStruct((SLOTS // 128, 128), F32),
        ),
        in_specs=[anywhere, anywhere, vmem, smem, vmem, vmem, vmem, smem],
        out_specs=(anywhere, vmem, anywhere, vmem),
        scratch_shapes=[
            pltpu.VMEM((W, ROWS), F32),
            pltpu.VMEM((W, RELS), F32),
            pltpu.VMEM((2 * W + 16, ROWS), BF16),
            pltpu.VMEM((W, RELS), BF16),
            pltpu.VMEM((16, ROWS), F32),
            pltpu.VMEM((8, GROUP), I32),
            pltpu.VMEM((2, 8, GROUP), I32),
            pltpu.VMEM((4, 8, GROUP), I32),
            pltpu.VMEM((4, 4 * GROUP, 1), F32),
            blocks, blocks, blocks,
            contributions, contributions,
            pltpu.VMEM((W, 2 * GROUP), F32),
            pltpu.VMEM((W, SHARE), F32),
            pltpu.VMEM((8, SHARE), F32),
            pltpu.VMEM((W, SLOTS), F32),
            pltpu.VMEM((W, SLOTS), BF16),
            pltpu.VMEM((W, FIRST), BF16),
            pltpu.VMEM((W, SECOND), BF16),
            pltpu.VMEM((3, W, 256), BF16),
            pltpu.VMEM((W, 256), F32),
            pltpu.VMEM((SECOND, WIDE), F32),
            pltpu.VMEM((7, PER_1, WIDE), BF16),
            pltpu.VMEM((4, PER_1, WIDE), BF16),
            pltpu.VMEM((4, PER_1, WIDE), BF16),
            pltpu.VMEM((PER_1, 128), F32),
            pltpu.VMEM((SECOND, WIDE), BF16),
            pltpu.VMEM((SECOND, WIDE), BF16),
            pltpu.VMEM((TALL, SLOTS), BF16),
            pltpu.SemaphoreType.DMA((7,)),
            pltpu.SemaphoreType.DMA((SEMS,)),
            pltpu.SemaphoreType.DMA((SEMS,)),
        ],
        compiler_params=pltpu.CompilerParams(
            collective_id=0, has_side_effects=True, vmem_limit_bytes=60 * 1024 * 1024
        ),
    )(
        entity_table.T, relation_table.T, entity_state.reshape(ROWS // 128, 128), relation_state,
        source_rows, target_rows, relation_ids, live_counts.reshape(-1),
    )
    new_state = relation_state + mean.reshape(-1)[:RELS]
    return own.T, own_state.reshape(-1), new_relations.T, new_state


def solution(mesh):
    in_specs = (
        P("dom", None),
        P("dom"),
        P(),
        P(),
        P(None, "dom", "rep"),
        P(None, "dom", "rep"),
        P(None, "dom", "rep"),
        P(None, "dom", "rep"),
    )
    out_specs = (P(("dom", "rep"), None), P(("dom", "rep")), P(), P())
    return jax.shard_map(per_device, mesh=mesh, in_specs=in_specs, out_specs=out_specs, check_vma=False)
```

```python
import jax
import jax.numpy as jnp
from jax import lax
from jax.experimental import pallas as pl
from jax.experimental.pallas import tpu as pltpu
from jax.sharding import PartitionSpec as P

MESH = pl.DeviceIdType.MESH
F32, BF16, I32 = jnp.float32, jnp.bfloat16, jnp.int32

RATE = 0.2
EPS = 1e-06
W = 400
HALF = 200
TALL = 416
WIDE = 512
ROWS = 4096
SHARE = 1024
GROUP = 256
RELS = 1300
HALF_SLOTS = 768
SLOTS = 2 * HALF_SLOTS
FIRST_PART, SECOND_PART, THIRD_PART = 192, 48, 16
PIECES = ((0, 208), (208, 192))
SEMS = 112


def mat(a, b):
    return jnp.dot(a, b, preferred_element_type=F32)


def iota(shape, dim):
    return lax.broadcasted_iota(I32, shape, dim)


def indicator(hit):
    return jnp.where(hit, 1.0, 0.0).astype(BF16)


def columns(rows):
    eye = indicator(iota((GROUP, GROUP), 0) == iota((GROUP, GROUP), 1))

    def turned(part):
        return lax.dot_general(
            eye, part.astype(F32).astype(BF16), (((1,), (1,)), ((), ())), preferred_element_type=F32
        )

    return turned(lax.shift_right_logical(rows, 8)) * 256.0 + turned(jnp.bitwise_and(rows, 255))


def adagrad(rows, state, grads):
    state = state + jnp.sum(grads * grads, axis=0, keepdims=True) * (1.0 / W)
    return rows - RATE * grads / (jnp.sqrt(state) + EPS), state


def kernel(
    tab_hbm, rtab_hbm, state_v, rstate_s, src_v, tgt_v, rid_v, live_s,
    own, est_ref, delta_ref,
    tab, rtab, parts, rtab_b, st_parts, msg, idx_in, comb, cid,
    out_rows, rows_in, back, c0, c1, gsum, req1, src1, req1_st, src1_st, rel1, drel, own_st,
    h0, hsend, dmate, xin, qsum, qsend, sin, rsum, rsend, zin, rst, dall,
    local_sem, send_sem, recv_sem,
):
    dom, rep = lax.axis_index("dom"), lax.axis_index("rep")
    core, y_lo = lax.rem(rep, 2), lax.div(rep, 2)
    x, z, y_hi = lax.rem(dom, 4), lax.rem(lax.div(dom, 4), 8), lax.div(dom, 32)
    y = 2 * y_hi + y_lo
    plane = 32 * y_hi

    core_rep, y_rep = rep + 1 - 2 * core, lax.rem(rep + 2, 4)
    core_mate, y_mate = (dom, core_rep), (dom, y_rep)
    cross_mate = (dom, y_rep + 1 - 2 * core)
    after = (lax.rem(dom + 1, 64), rep)
    before = (lax.rem(dom + 63, 64), rep)
    before_y, after_y = (lax.rem(dom + 63, 64), y_rep), (lax.rem(dom + 1, 64), y_rep)
    other = (lax.rem(dom + 32, 64), y_rep)
    opposite = (lax.rem(dom + 32, 64), rep)
    x_peers = [(plane + 4 * z + lax.rem(x + k, 4), rep) for k in range(1, 4)]
    z_peers = [(plane + 4 * lax.rem(z + k, 8) + x, rep) for k in range(1, 8)]

    def beside(in_x, in_y):
        y_there = lax.rem(y + in_y, 4)
        return 32 * lax.div(y_there, 2) + 4 * z + lax.rem(x + in_x, 4), 2 * lax.rem(y_there, 2) + core

    first_peers = [beside((1 - core) * k, core * k) for k in range(1, 4)]
    second_peers = [beside(core * k, (1 - core) * k) for k in range(1, 4)]
    first, second = (1 - core) * x + core * y, core * x + (1 - core) * y
    mine_from = core * HALF_SLOTS

    def third(k):
        place = lax.rem(z + 4 * core + k + 8, 8)
        return lax.rem(place, 3) == 0, lax.div(place, 3)

    count = [0]

    def send(src, dst, device):
        i = count[0]
        count[0] += 1
        assert i < SEMS
        return pltpu.make_async_remote_copy(
            src_ref=src, dst_ref=dst, send_sem=send_sem.at[i], recv_sem=recv_sem.at[i],
            device_id=device, device_id_type=MESH,
        )

    def start(copies):
        for copy in copies:
            copy.start()

    def lanes(ref, lo, size):
        return ref.at[:, pl.ds(pl.multiple_of(lo, 128), size)]

    def at_rows(ref, lo, size):
        return ref.at[pl.ds(pl.multiple_of(lo, 16), size), :]

    loads = [
        pltpu.make_async_copy(lanes(tab_hbm, k * 1024, 1024), lanes(tab, k * 1024, 1024), local_sem.at[k])
        for k in range(4)
    ]
    start(loads)
    load_rtab = pltpu.make_async_copy(rtab_hbm, rtab, local_sem.at[4])
    load_rtab.start()

    barrier = pltpu.get_barrier_semaphore()
    greeted = [core_mate, y_mate, cross_mate, after, before, after_y, before_y, other, opposite] + x_peers + z_peers
    for device in greeted:
        pl.semaphore_signal(barrier, inc=1, device_id=device, device_id_type=MESH)
    for t in range(2):
        msg[t : t + 1, :] = src_v[t]
        msg[2 + t : 3 + t, :] = tgt_v[t]
        msg[4 + t : 5 + t, :] = rid_v[t]
    msg[6:8, :] = jnp.full((2, GROUP), live_s[0], I32)
    pl.semaphore_wait(barrier, len(greeted))

    ask0 = send(msg, idx_in.at[0], after)
    ask1 = send(msg, idx_in.at[1], other)
    start([ask0, ask1])

    def lookup(table, ids):
        return mat(table, indicator(iota((table.shape[1], GROUP), 0) == ids))

    def high(k, carry):
        at = pl.ds(pl.multiple_of(k * 256, 256), 256)
        parts[0:W, at] = tab[:, at].astype(BF16)
        return carry

    for k in range(4):
        loads[k].wait()
        lax.fori_loop(4 * k, 4 * k + 4, high, 0)

    out_rows[0] = lookup(parts[0:W, :], msg[0:1, :]).astype(BF16)
    rows_out0 = send(out_rows.at[0], rows_in.at[0], after)
    rows_out0.start()

    def product(a, b):
        return jnp.concatenate(
            [a[:HALF] * b[:HALF] - a[HALF:] * b[HALF:], a[:HALF] * b[HALF:] + a[HALF:] * b[:HALF]], axis=0
        )

    def conj_product(a, b):
        return jnp.concatenate(
            [a[:HALF] * b[:HALF] + a[HALF:] * b[HALF:], a[HALF:] * b[:HALF] - a[:HALF] * b[HALF:]], axis=0
        )

    def coefficients(queries_row, tgt, live):
        scores = mat(queries_row, tgt)
        row_id, col_id = iota((GROUP, GROUP), 0), iota((GROUP, GROUP), 1)
        terms = jnp.where(col_id < live, jnp.exp(scores), 0.0)
        probs = terms / jnp.sum(terms, axis=1, keepdims=True)
        return jnp.where(row_id < live, probs - jnp.where(row_id == col_id, 1.0, 0.0), 0.0)

    def block_at(ref, holder, kind, piece):
        lo, size = PIECES[piece]
        return ref.at[pl.ds(lo, size), pl.ds(pl.multiple_of(kind * 1024 + holder * GROUP, GROUP), GROUP)]

    def share_in_rep(ref, kind, piece):
        mine, got = block_at(ref, rep, kind, piece), block_at(ref, y_rep, kind, piece)
        return send(mine, mine, core_mate), send(mine, mine, y_mate), send(got, got, core_mate)

    def back_copies(t, ref, to, kind):
        return [
            send(back.at[t, pl.ds(lo, size), :], block_at(ref, to[1], kind, k), to)
            for k, (lo, size) in enumerate(PIECES)
        ]

    def share_copies(ref):
        return [[share_in_rep(ref, kind, k) for k in range(len(PIECES))] for kind in range(2)]

    def mine_at(kind):
        return pl.ds(pl.multiple_of(kind * 1024 + rep * GROUP, GROUP), GROUP)

    ask0.wait_recv()
    tgt0 = lookup(parts[0:W, :], idx_in[0, 2:3, :]).astype(BF16)
    load_rtab.wait()
    rtab_b[...] = rtab[...].astype(BF16)
    rel0 = lookup(rtab_b[...], idx_in[0, 4:5, :])
    backs0, shares0 = back_copies(0, c0, before, 0), share_copies(c0)[1]
    backs0_y = [
        send(back.at[0, pl.ds(lo, size), :], block_at(c0, rep, 0, k), before_y)
        for k, (lo, size) in enumerate(PIECES)
    ]
    pass_on = [
        [send(block_at(c0, holder, 0, k), block_at(c0, holder, 0, k), core_mate) for holder in (rep, y_rep)]
        for k in range(len(PIECES))
    ]
    rows_out0.wait_recv()
    src0 = rows_in[0].astype(F32)
    queries = product(src0, rel0)
    coeffs = coefficients(queries.T.astype(BF16), tgt0, idx_in[0, 6:7, :])
    d_queries = mat(tgt0, coeffs.T.astype(BF16))
    back[0] = conj_product(d_queries, rel0).astype(BF16)
    for k in range(len(PIECES)):
        backs0[k].start()
        backs0_y[k].start()
    c0[:, mine_at(1)] = mat(queries.astype(BF16), coeffs.astype(BF16)).astype(BF16)
    for group in shares0:
        start(group[:2])
    drel[...] = jnp.zeros(drel.shape, BF16)
    drel[0, :, 0:W] = conj_product(d_queries, src0).T.astype(BF16)
    drel_sends = [send(drel.at[t], dmate.at[t], core_mate) for t in range(2)]
    drel_sends[0].start()

    ask1.wait_recv()
    comb[rep, 0:2, :] = msg[0:2, :]
    comb[rep, 2:3, :] = idx_in[0, 2:3, :]
    comb[rep, 3:4, :] = idx_in[1, 3:4, :]
    comb[rep, 4:5, :] = idx_in[0, 4:5, :]
    comb[rep, 5:6, :] = msg[5:6, :]
    comb[rep, 6:8, :] = jnp.zeros((2, GROUP), I32)
    combs = [send(comb.at[rep], comb.at[rep], device) for device in (core_mate, y_mate, cross_mate)]
    start(combs)

    def low(k, carry):
        at = pl.ds(pl.multiple_of(k * 256, 256), 256)
        parts[W : 2 * W, at] = (tab[:, at] - parts[0:W, at].astype(F32)).astype(BF16)
        return carry

    lax.fori_loop(0, ROWS // 256, low, 0)
    st_parts[...] = jnp.zeros(st_parts.shape, F32)
    for k in range(ROWS // 128):
        whole = state_v[k : k + 1, :]
        top = whole.astype(BF16).astype(F32)
        mid = (whole - top).astype(BF16).astype(F32)
        st_parts[0:1, k * 128 : (k + 1) * 128] = top
        st_parts[1:2, k * 128 : (k + 1) * 128] = mid
        st_parts[2:3, k * 128 : (k + 1) * 128] = whole - top - mid
    parts[2 * W : 2 * W + 16, :] = st_parts[...].astype(BF16)

    def lookup_f32(ids, rows, state):
        got = lookup(parts[...], ids)
        state[0:1, :] = got[2 * W : 2 * W + 1] + got[2 * W + 1 : 2 * W + 2] + got[2 * W + 2 : 2 * W + 3]
        rows[...] = got[0:W] + got[W : 2 * W]

    req1_ids, src1_ids = idx_in[1, 3:4, :], msg[1:2, :]
    lookup_f32(req1_ids, req1, req1_st)

    for k in range(len(PIECES)):
        shares0[k][1].wait_recv()
        shares0[k][2].start()

    lookup_f32(src1_ids, src1, src1_st)
    for copy in combs:
        copy.wait_recv()
    for b in range(4):
        turned = columns(comb[b])
        for q in range(4):
            cid[q, b * GROUP : (b + 1) * GROUP, :] = turned[:, q : q + 1]
    for k in range(len(PIECES)):
        backs0[k].wait_recv()
        pass_on[k][0].start()
        backs0_y[k].wait_recv()
        pass_on[k][1].start()
    for group in shares0:
        group[0].wait_recv()
        group[2].wait_recv()

    def summed(ref, kind, q, ids):
        return mat(ref[:, kind * 1024 : (kind + 1) * 1024], indicator(cid[q] == ids.astype(F32)))

    own_first = rep * SHARE

    def tile_ids(tile):
        return iota((1, GROUP), 1) + (own_first + tile * GROUP)

    gsum[:, 0:256] = summed(c0, 1, 2, req1_ids)
    gsum[:, 256:512] = summed(c0, 1, 2, src1_ids)
    def relation_part(t, rows, rid, lo):
        ids = iota((FIRST_PART, 1), 0) + (mine_from + lo)
        return mat(indicator(ids == rid), rows[t])

    drel_sends[0].wait_recv()
    for lo in range(0, HALF_SLOTS, FIRST_PART):
        h0[lo : lo + FIRST_PART, :] = relation_part(0, drel, idx_in[0, 4:5, :], lo) + relation_part(
            0, dmate, comb[core_rep, 4:5, :], lo
        )
    rel1[...] = lookup(rtab_b[...], msg[5:6, :])

    for group in pass_on:
        for copy in group:
            copy.wait_recv()

    def updated(rows, state, at, ids):
        grads = gsum[:, at] + summed(c0, 0, 0, ids)
        return adagrad(rows[...], state[0:1, :], grads)[0].astype(BF16)

    out_rows[1] = updated(req1, req1_st, slice(0, 256), req1_ids)
    rows_out1 = send(out_rows.at[1], rows_in.at[1], other)
    rows_out1.start()
    src1_b = updated(src1, src1_st, slice(256, 512), src1_ids)
    src1[...] = src1_b.astype(F32)
    queries = product(src1[...], rel1[...])
    queries_row, queries_b = queries.T.astype(BF16), queries.astype(BF16)

    sums_third, my_third = third(0)
    second_row = pl.multiple_of(mine_from + first * FIRST_PART + second * SECOND_PART, 16)
    third_row = pl.multiple_of(second_row + my_third * THIRD_PART, 16)
    for k in range(THIRD_PART):
        rst[k : k + 1, :] = jnp.full((1, 128), rstate_s[jnp.minimum(third_row + k, RELS - 1)], F32)
    for k in range(8):
        own_st[0:1, k * 128 : (k + 1) * 128] = state_v[pl.ds(rep * 8 + k, 1), :]

    for tile in range(SHARE // GROUP):
        at = slice(tile * GROUP, (tile + 1) * GROUP)
        grads = summed(c0, 0, 0, tile_ids(tile)) + summed(c0, 1, 2, tile_ids(tile))
        rows = tab[:, pl.ds(pl.multiple_of(own_first + tile * GROUP, GROUP), GROUP)]
        own[:, at], own_st[0:1, at] = adagrad(rows, own_st[0:1, at], grads)

    rows_out1.wait_recv()
    backs1, shares1 = back_copies(1, c1, other, 1), share_copies(c1)
    coeffs = coefficients(queries_row, rows_in[1], live_s[1])
    d_queries = mat(rows_in[1], coeffs.T.astype(BF16))
    drel[1, :, 0:W] = conj_product(d_queries, src1[...]).T.astype(BF16)

    drel_sends[1].start()

    def quarter(ref, lo):
        return at_rows(ref, lo, FIRST_PART)

    my_lo = [lax.rem(first + k, 4) * FIRST_PART for k in (1, 2, 3, 0)]
    firsts = [send(quarter(hsend, my_lo[k]), xin.at[k], first_peers[k]) for k in range(3)]
    for lo in my_lo:
        quarter(h0, lo)[...] += relation_part(1, drel, msg[5:6, :], lo)
    drel_sends[1].wait_recv()
    for k in range(4):
        total = quarter(h0, my_lo[k])[...] + relation_part(1, dmate, comb[core_rep, 5:6, :], my_lo[k])
        if k < 3:
            quarter(hsend, my_lo[k])[...] = total.astype(BF16)
            firsts[k].start()
        else:
            qsum[...] = total

    back[1] = mat(queries_b, coeffs.astype(BF16)).astype(BF16)
    start(backs1)
    c1[:, mine_at(0)] = conj_product(d_queries, rel1[...]).astype(BF16)
    for group in shares1[0]:
        start(group[:2])

    for k in range(3):
        firsts[k].wait_recv()
        qsum[...] += xin[k].astype(F32)
    qsend[...] = qsum[...].astype(BF16)

    seconds = [
        send(at_rows(qsend, lax.rem(second + k, 4) * SECOND_PART, SECOND_PART), sin.at[k - 1], second_peers[k - 1])
        for k in range(1, 4)
    ]
    start(seconds)
    for k in range(len(PIECES)):
        backs1[k].wait_recv()
        start(shares1[1][k][:2])
    total = at_rows(qsum, second * SECOND_PART, SECOND_PART)[...]
    for k in range(3):
        seconds[k].wait_recv()
        total = total + sin[k].astype(F32)
    rsum[...] = total
    rsend[...] = total.astype(BF16)

    thirds = [
        send(at_rows(rsend, third(k)[1] * THIRD_PART, THIRD_PART), zin.at[k - 1], z_peers[k - 1])
        for k in range(1, 8)
    ]
    for k in range(1, 8):
        pl.when(third(k)[0])(thirds[k - 1].start)
    for k in range(len(PIECES)):
        shares1[0][k][1].wait_recv()
        shares1[0][k][2].start()

    third_rows = at_rows(dall, third_row, THIRD_PART)
    out_z = [send(third_rows, third_rows, device) for device in z_peers]

    @pl.when(sums_third)
    def _():
        total = at_rows(rsum, my_third * THIRD_PART, THIRD_PART)[...]
        for k in range(7):
            thirds[k].wait_recv()
            total = total + zin[k].astype(F32)
        mean = jnp.sum(total * total, axis=1, keepdims=True) * (1.0 / W)
        delta = -RATE * total / (jnp.sqrt(rst[:, 0:1] + mean) + EPS)
        mean_hi = mean.astype(BF16).astype(F32)
        lane = iota((THIRD_PART, WIDE), 1)
        delta = jnp.where(lane == W, mean_hi, jnp.where(lane == W + 1, mean - mean_hi, delta))
        third_rows[...] = delta.astype(BF16)
        start(out_z)

    for group in shares1[1]:
        group[1].wait_recv()
        group[2].start()
    for kind in range(2):
        for group in shares1[kind]:
            group[0].wait_recv()
            group[2].wait_recv()

    def own_tiles(tiles):
        for tile in tiles:
            at = slice(tile * GROUP, (tile + 1) * GROUP)
            grads = summed(c1, 0, 1, tile_ids(tile)) + summed(c1, 1, 3, tile_ids(tile))
            own[:, at], own_st[0:1, at] = adagrad(own[:, at], own_st[0:1, at], grads)

    own_tiles((0,))
    for k in range(1, 8):
        pl.when(third(-k)[0])(out_z[k - 1].wait_recv)
    second_rows = at_rows(dall, second_row, SECOND_PART)
    out_second = [send(second_rows, second_rows, device) for device in second_peers]
    start(out_second)
    own_tiles((1,))
    for copy in out_second:
        copy.wait_recv()
    first_rows = quarter(dall, mine_from + first * FIRST_PART)
    out_first = [send(first_rows, first_rows, device) for device in first_peers]
    start(out_first)
    swaps = [send(first_rows, first_rows, core_mate)]
    for k in range(1, 4):
        got = quarter(dall, mine_from + lax.rem(first + 4 - k, 4) * FIRST_PART)
        swaps.append(send(got, got, core_mate))
    swaps[0].start()
    own_tiles((2, 3))
    for k in range(8):
        est_ref[k : k + 1, :] = own_st[0:1, k * 128 : (k + 1) * 128]
    for k in range(3):
        out_first[k].wait_recv()
        swaps[k + 1].start()

    def turn(lo):
        lo = pl.multiple_of(lo, 128)
        delta_ref[:, pl.ds(lo, HALF_SLOTS)] = dall[pl.ds(lo, HALF_SLOTS), :].astype(F32).T[0:TALL].astype(BF16)

    turn(mine_from)
    for copy in swaps:
        copy.wait_recv()
    turn((1 - core) * HALF_SLOTS)

    for copy in [ask0, ask1, rows_out0, rows_out1] + combs + backs0 + backs0_y + backs1 + drel_sends:
        copy.wait_send()
    for group in shares0 + pass_on + shares1[0] + shares1[1]:
        for copy in group:
            copy.wait_send()
    for copy in firsts + seconds + out_second + out_first + swaps:
        copy.wait_send()
    for k in range(1, 8):
        pl.when(third(k)[0])(thirds[k - 1].wait_send)

    @pl.when(sums_third)
    def _():
        for copy in out_z:
            copy.wait_send()


OWN_PIECES = ((0, 104), (104, 104), (208, 96), (304, 96))


def finish(own, own_state, delta, rtab, rstate, ent_hbm, est_ref, rel_hbm, nstate, total, sem):
    def pieces(source, target, first):
        return [
            pltpu.make_async_copy(source.at[pl.ds(lo, size), :], target.at[pl.ds(lo, size), :], sem.at[first + k])
            for k, (lo, size) in enumerate(OWN_PIECES)
        ]

    stores, rel_stores = pieces(own, ent_hbm, 0), pieces(total, rel_hbm, 4)
    for store in stores:
        store.start()
    for k, (lo, size) in enumerate(OWN_PIECES):
        at = slice(lo, lo + size)
        total[at, :] = rtab[at, :] + delta[at, 0:RELS].astype(F32)
        rel_stores[k].start()
    est_ref[...] = own_state[...]
    tail = delta[W:TALL, :].astype(F32)
    mean = tail[0:1, :] + tail[1:2, :]
    nstate[...] = rstate[...] + mean.reshape(SLOTS)[:RELS]
    for store in stores + rel_stores:
        store.wait()


def per_device(
    entity_table, entity_state, relation_table, relation_state, source_rows, target_rows, relation_ids, live_counts
):
    vmem, smem = pl.BlockSpec(memory_space=pltpu.VMEM), pl.BlockSpec(memory_space=pltpu.SMEM)
    anywhere = pl.BlockSpec(memory_space=pl.ANY)
    contributions = pltpu.VMEM((W, 8 * GROUP), BF16)
    blocks = pltpu.VMEM((2, W, GROUP), BF16)
    block_f, state_row = pltpu.VMEM((W, GROUP), F32), pltpu.VMEM((8, GROUP), F32)
    relations = relation_table.T
    own, own_state, delta = pl.pallas_call(
        kernel,
        out_shape=(
            pltpu.VMEM((W, SHARE), F32),
            pltpu.VMEM((8, 128), F32),
            pltpu.VMEM((TALL, SLOTS), BF16),
        ),
        in_specs=[anywhere, anywhere, vmem, smem, vmem, vmem, vmem, smem],
        out_specs=(vmem, vmem, vmem),
        scratch_shapes=[
            pltpu.VMEM((W, ROWS), F32),
            pltpu.VMEM((W, RELS), F32),
            pltpu.VMEM((2 * W + 16, ROWS), BF16),
            pltpu.VMEM((W, RELS), BF16),
            pltpu.VMEM((16, ROWS), F32),
            pltpu.VMEM((8, GROUP), I32),
            pltpu.VMEM((2, 8, GROUP), I32),
            pltpu.VMEM((4, 8, GROUP), I32),
            pltpu.VMEM((4, 4 * GROUP, 1), F32),
            blocks, blocks, blocks,
            contributions, contributions,
            pltpu.VMEM((W, 2 * GROUP), F32),
            block_f, block_f, state_row, state_row, block_f,
            pltpu.VMEM((2, GROUP, WIDE), BF16),
            pltpu.VMEM((8, SHARE), F32),
            pltpu.VMEM((HALF_SLOTS, WIDE), F32),
            pltpu.VMEM((HALF_SLOTS, WIDE), BF16),
            pltpu.VMEM((2, GROUP, WIDE), BF16),
            pltpu.VMEM((3, FIRST_PART, WIDE), BF16),
            pltpu.VMEM((FIRST_PART, WIDE), F32),
            pltpu.VMEM((FIRST_PART, WIDE), BF16),
            pltpu.VMEM((3, SECOND_PART, WIDE), BF16),
            pltpu.VMEM((SECOND_PART, WIDE), F32),
            pltpu.VMEM((SECOND_PART, WIDE), BF16),
            pltpu.VMEM((7, THIRD_PART, WIDE), BF16),
            pltpu.VMEM((THIRD_PART, 128), F32),
            pltpu.VMEM((SLOTS, WIDE), BF16),
            pltpu.SemaphoreType.DMA((7,)),
            pltpu.SemaphoreType.DMA((SEMS,)),
            pltpu.SemaphoreType.DMA((SEMS,)),
        ],
        compiler_params=pltpu.CompilerParams(
            collective_id=0, has_side_effects=True, vmem_limit_bytes=58 * 1024 * 1024
        ),
    )(
        entity_table.T, relations, entity_state.reshape(ROWS // 128, 128), relation_state,
        source_rows, target_rows, relation_ids, live_counts.reshape(-1),
    )
    own, own_state, new_relations, new_state = pl.pallas_call(
        finish,
        out_shape=(
            jax.ShapeDtypeStruct((W, SHARE), F32),
            jax.ShapeDtypeStruct((8, 128), F32),
            jax.ShapeDtypeStruct((W, RELS), F32),
            jax.ShapeDtypeStruct((RELS,), F32),
        ),
        in_specs=[vmem, vmem, vmem, vmem, vmem],
        out_specs=(anywhere, vmem, anywhere, vmem),
        scratch_shapes=[
            pltpu.VMEM((W, RELS), F32),
            pltpu.SemaphoreType.DMA((8,)),
        ],
        compiler_params=pltpu.CompilerParams(vmem_limit_bytes=12 * 1024 * 1024),
    )(own, own_state, delta, relations, relation_state)
    return own.T, own_state.reshape(-1), new_relations.T, new_state


def solution(mesh):
    in_specs = (
        P("dom", None),
        P("dom"),
        P(),
        P(),
        P(None, "dom", "rep"),
        P(None, "dom", "rep"),
        P(None, "dom", "rep"),
        P(None, "dom", "rep"),
    )
    out_specs = (P(("dom", "rep"), None), P(("dom", "rep")), P(), P())
    return jax.shard_map(per_device, mesh=mesh, in_specs=in_specs, out_specs=out_specs, check_vma=False)
```

```python
import functools

import jax
import jax.numpy as jnp
from jax import lax
from jax.experimental import pallas as pl
from jax.experimental.pallas import tpu as pltpu
from jax.sharding import PartitionSpec as P

MESH = pl.DeviceIdType.MESH
F32, BF16, I32 = jnp.float32, jnp.bfloat16, jnp.int32

RATE = 0.2
EPS = 1e-06
W = 400
HALF = 200
TALL = 416
WIDE = 512
ROWS = 4096
SHARE = 1024
GROUP = 256
RELS = 1300
HALF_SLOTS = 768
SLOTS = 2 * HALF_SLOTS
FIRST_PART, CHAIN, THIRD_PART = 192, 64, 16
CHAINS = 3
PIECES = ((0, 208), (208, 192))
SEMS = 128


def mat(a, b):
    return jnp.dot(a, b, preferred_element_type=F32)


def iota(shape, dim):
    return lax.broadcasted_iota(I32, shape, dim)


def indicator(hit):
    return jnp.where(hit, 1.0, 0.0).astype(BF16)


def columns(rows):
    eye = indicator(iota((GROUP, GROUP), 0) == iota((GROUP, GROUP), 1))

    def turned(part):
        return lax.dot_general(
            eye, part.astype(F32).astype(BF16), (((1,), (1,)), ((), ())), preferred_element_type=F32
        )

    return turned(lax.shift_right_logical(rows, 8)) * 256.0 + turned(jnp.bitwise_and(rows, 255))


def adagrad(rows, state, grads):
    state = state + jnp.sum(grads * grads, axis=0, keepdims=True) * (1.0 / W)
    return rows - RATE * grads / (jnp.sqrt(state) + EPS), state


def kernel(
    tab_hbm, rtab_hbm, state_hbm, rstate_hbm, src_hbm, tgt_hbm, rid_hbm, live_hbm,
    own, est_ref, rtab, mean_ref,
    tab, parts, rtab_b, st_parts, state_v, rstate_s, src_v, tgt_v, rid_v, live_s, msg, idx_in, comb, cid,
    out_rows, rows_in, back, c0, c1, gsum, req1, src1, req1_st, src1_st, rel1, drel, own_st,
    h0, hsend, dmate, xin, qsum, qsend, sin, rsum, rsend, zin, rst, dall,
    local_sem, send_sem, recv_sem,
):
    dom, rep = lax.axis_index("dom"), lax.axis_index("rep")
    core, y_lo = lax.rem(rep, 2), lax.div(rep, 2)
    x, z, y_hi = lax.rem(dom, 4), lax.rem(lax.div(dom, 4), 8), lax.div(dom, 32)
    y = 2 * y_hi + y_lo
    plane = 32 * y_hi

    core_rep, y_rep = rep + 1 - 2 * core, lax.rem(rep + 2, 4)
    core_mate, y_mate = (dom, core_rep), (dom, y_rep)
    cross_mate = (dom, y_rep + 1 - 2 * core)
    after = (lax.rem(dom + 1, 64), rep)
    before = (lax.rem(dom + 63, 64), rep)
    before_y, after_y = (lax.rem(dom + 63, 64), y_rep), (lax.rem(dom + 1, 64), y_rep)
    other = (lax.rem(dom + 32, 64), y_rep)
    opposite = (lax.rem(dom + 32, 64), rep)
    x_peers = [(plane + 4 * z + lax.rem(x + k, 4), rep) for k in range(1, 4)]
    z_peers = [(plane + 4 * lax.rem(z + k, 8) + x, rep) for k in range(1, 8)]

    def beside(in_x, in_y):
        y_there = lax.rem(y + in_y, 4)
        return 32 * lax.div(y_there, 2) + 4 * z + lax.rem(x + in_x, 4), 2 * lax.rem(y_there, 2) + core

    first_peers = [beside((1 - core) * k, core * k) for k in range(1, 4)]
    second_peers = [beside(core * k, (1 - core) * k) for k in range(1, 4)]
    first, second = (1 - core) * x + core * y, core * x + (1 - core) * y
    mine_from = core * HALF_SLOTS

    def third(k):
        place = lax.rem(z + 4 * core + k + 8, 8)
        return lax.rem(place, 3) == 0, lax.div(place, 3)

    def holds(k, t):
        return lax.rem(z + 4 * core + k + 8, 8) == 3 * t

    count = [0]

    def send(src, dst, device):
        i = count[0]
        count[0] += 1
        assert i < SEMS
        return pltpu.make_async_remote_copy(
            src_ref=src, dst_ref=dst, send_sem=send_sem.at[i], recv_sem=recv_sem.at[i],
            device_id=device, device_id_type=MESH,
        )

    def start(copies):
        for copy in copies:
            copy.start()

    def lanes(ref, lo, size):
        return ref.at[:, pl.ds(pl.multiple_of(lo, 128), size)]

    def at_rows(ref, lo, size):
        return ref.at[pl.ds(pl.multiple_of(lo, 16), size), :]

    loads = [
        pltpu.make_async_copy(lanes(tab_hbm, k * 1024, 1024), lanes(tab, k * 1024, 1024), local_sem.at[k])
        for k in range(4)
    ]
    smalls = [
        pltpu.make_async_copy(source, target, local_sem.at[5 + k])
        for k, (source, target) in enumerate(
            (
                (src_hbm, src_v), (tgt_hbm, tgt_v), (rid_hbm, rid_v), (live_hbm, live_s),
                (state_hbm, state_v), (rstate_hbm, rstate_s),
            )
        )
    ]
    start(smalls)
    start(loads)
    load_rtab = pltpu.make_async_copy(rtab_hbm, rtab, local_sem.at[4])

    barrier = pltpu.get_barrier_semaphore()
    greeted = [core_mate, y_mate, cross_mate, after, before, after_y, before_y, other, opposite] + x_peers + z_peers
    for device in greeted:
        pl.semaphore_signal(barrier, inc=1, device_id=device, device_id_type=MESH)
    for copy in smalls:
        copy.wait()
    for t in range(2):
        msg[t : t + 1, :] = src_v[t]
        msg[2 + t : 3 + t, :] = tgt_v[t]
        msg[4 + t : 5 + t, :] = rid_v[t]
    msg[6:8, :] = jnp.full((2, GROUP), live_s[0], I32)
    pl.semaphore_wait(barrier, len(greeted))

    ask0 = send(msg, idx_in.at[0], after)
    ask1 = send(msg, idx_in.at[1], other)
    start([ask0, ask1])

    def lookup(table, ids):
        return mat(table, indicator(iota((table.shape[1], GROUP), 0) == ids))

    st_parts[...] = jnp.zeros(st_parts.shape, F32)
    for k in range(ROWS // 128):
        whole = state_v[k : k + 1, :]
        top = whole.astype(BF16).astype(F32)
        mid = (whole - top).astype(BF16).astype(F32)
        st_parts[0:1, k * 128 : (k + 1) * 128] = top
        st_parts[1:2, k * 128 : (k + 1) * 128] = mid
        st_parts[2:3, k * 128 : (k + 1) * 128] = whole - top - mid
    parts[W : W + 16, :] = st_parts[...].astype(BF16)

    sums_third, my_third = third(0)
    first_row = mine_from + first * FIRST_PART
    third_row = pl.multiple_of(first_row + my_third * CHAIN + second * THIRD_PART, 16)
    for k in range(THIRD_PART):
        rst[k : k + 1, :] = jnp.full((1, 128), rstate_s[jnp.minimum(third_row + k, RELS - 1)], F32)
    for k in range(8):
        own_st[0:1, k * 128 : (k + 1) * 128] = state_v[pl.ds(rep * 8 + k, 1), :]

    drel[...] = jnp.zeros(drel.shape, BF16)

    def high(k, carry):
        at = pl.ds(pl.multiple_of(k * 256, 256), 256)
        parts[0:W, at] = tab[:, at].astype(BF16)
        return carry

    for k in range(4):
        loads[k].wait()
        lax.fori_loop(4 * k, 4 * k + 4, high, 0)
    load_rtab.start()

    out_rows[0] = lookup(parts[0:W, :], msg[0:1, :]).astype(BF16)
    rows_out0 = send(out_rows.at[0], rows_in.at[0], after)
    rows_out0.start()

    def product(a, b):
        return jnp.concatenate(
            [a[:HALF] * b[:HALF] - a[HALF:] * b[HALF:], a[:HALF] * b[HALF:] + a[HALF:] * b[:HALF]], axis=0
        )

    def conj_product(a, b):
        return jnp.concatenate(
            [a[:HALF] * b[:HALF] + a[HALF:] * b[HALF:], a[HALF:] * b[:HALF] - a[:HALF] * b[HALF:]], axis=0
        )

    def coefficients(queries_row, tgt, live):
        scores = mat(queries_row, tgt)
        row_id, col_id = iota((GROUP, GROUP), 0), iota((GROUP, GROUP), 1)
        terms = jnp.where(col_id < live, jnp.exp(scores), 0.0)
        probs = terms / jnp.sum(terms, axis=1, keepdims=True)
        return jnp.where(row_id < live, probs - jnp.where(row_id == col_id, 1.0, 0.0), 0.0)

    def block_at(ref, holder, kind, piece):
        lo, size = PIECES[piece]
        return ref.at[pl.ds(lo, size), pl.ds(pl.multiple_of(kind * 1024 + holder * GROUP, GROUP), GROUP)]

    def share_in_rep(ref, kind, piece):
        mine, got = block_at(ref, rep, kind, piece), block_at(ref, y_rep, kind, piece)
        return send(mine, mine, core_mate), send(mine, mine, y_mate), send(got, got, core_mate)

    def back_copies(t, ref, to, kind):
        return [
            send(back.at[t, pl.ds(lo, size), :], block_at(ref, to[1], kind, k), to)
            for k, (lo, size) in enumerate(PIECES)
        ]

    def share_copies(ref):
        return [[share_in_rep(ref, kind, k) for k in range(len(PIECES))] for kind in range(2)]

    def mine_at(kind):
        return pl.ds(pl.multiple_of(kind * 1024 + rep * GROUP, GROUP), GROUP)

    ask0.wait_recv()
    ask1.wait_recv()
    comb[rep, 0:2, :] = msg[0:2, :]
    comb[rep, 2:3, :] = idx_in[0, 2:3, :]
    comb[rep, 3:4, :] = idx_in[1, 3:4, :]
    comb[rep, 4:5, :] = idx_in[0, 4:5, :]
    comb[rep, 5:6, :] = msg[5:6, :]
    comb[rep, 6:8, :] = jnp.zeros((2, GROUP), I32)
    combs = [send(comb.at[rep], comb.at[rep], device) for device in (core_mate, y_mate, cross_mate)]
    start(combs)

    tgt0 = lookup(parts[0:W, :], idx_in[0, 2:3, :]).astype(BF16)
    load_rtab.wait()
    rtab_b[...] = rtab[...].astype(BF16)
    rel0 = lookup(rtab_b[...], idx_in[0, 4:5, :])

    def lookup_all(ids, rows, state):
        got = lookup(parts[...], ids)
        state[0:1, :] = got[W : W + 1] + got[W + 1 : W + 2] + got[W + 2 : W + 3]
        rows[...] = got[0:W]

    req1_ids, src1_ids = idx_in[1, 3:4, :], msg[1:2, :]
    lookup_all(req1_ids, req1, req1_st)

    backs0, shares0 = back_copies(0, c0, before, 0), share_copies(c0)[1]
    backs0_y = [
        send(back.at[0, pl.ds(lo, size), :], block_at(c0, rep, 0, k), before_y)
        for k, (lo, size) in enumerate(PIECES)
    ]
    pass_on = [
        [send(block_at(c0, holder, 0, k), block_at(c0, holder, 0, k), core_mate) for holder in (rep, y_rep)]
        for k in range(len(PIECES))
    ]
    rows_out0.wait_recv()
    src0 = rows_in[0].astype(F32)
    queries = product(src0, rel0)
    coeffs = coefficients(queries.T.astype(BF16), tgt0, idx_in[0, 6:7, :])
    d_queries = mat(tgt0, coeffs.T.astype(BF16))
    back[0] = conj_product(d_queries, rel0).astype(BF16)
    for k in range(len(PIECES)):
        backs0[k].start()
        backs0_y[k].start()
    c0[:, mine_at(1)] = mat(queries.astype(BF16), coeffs.astype(BF16)).astype(BF16)
    for group in shares0:
        start(group[:2])
    drel[0, :, 0:W] = conj_product(d_queries, src0).T.astype(BF16)
    drel_sends = [send(drel.at[t], dmate.at[t], core_mate) for t in range(2)]
    drel_sends[0].start()

    lookup_all(src1_ids, src1, src1_st)
    for copy in combs:
        copy.wait_recv()
    for b in range(4):
        turned = columns(comb[b])
        for q in range(4):
            cid[q, b * GROUP : (b + 1) * GROUP, :] = turned[:, q : q + 1]
    for k in range(len(PIECES)):
        shares0[k][1].wait_recv()
        shares0[k][2].start()

    for group in shares0:
        group[0].wait_recv()
        group[2].wait_recv()

    def summed(ref, kind, q, ids):
        return mat(ref[:, kind * 1024 : (kind + 1) * 1024], indicator(cid[q] == ids.astype(F32)))

    own_first = rep * SHARE

    def tile_ids(tile):
        return iota((1, GROUP), 1) + (own_first + tile * GROUP)

    gsum[:, 0:256] = summed(c0, 1, 2, req1_ids)
    gsum[:, 256:512] = summed(c0, 1, 2, src1_ids)

    def relation_part(t, rows, rid, lo):
        ids = iota((FIRST_PART, 1), 0) + (mine_from + lo)
        return mat(indicator(ids == rid), rows[t])

    drel_sends[0].wait_recv()
    for lo in range(0, HALF_SLOTS, FIRST_PART):
        h0[lo : lo + FIRST_PART, :] = relation_part(0, drel, idx_in[0, 4:5, :], lo) + relation_part(
            0, dmate, comb[core_rep, 4:5, :], lo
        )
    rel1[...] = lookup(rtab_b[...], msg[5:6, :])
    for k in range(len(PIECES)):
        backs0[k].wait_recv()
        pass_on[k][0].start()
        backs0_y[k].wait_recv()
        pass_on[k][1].start()

    for group in pass_on:
        for copy in group:
            copy.wait_recv()

    def updated(rows, state, at, ids):
        grads = gsum[:, at] + summed(c0, 0, 0, ids)
        return adagrad(rows[...], state[0:1, :], grads)[0].astype(BF16)

    out_rows[1] = updated(req1, req1_st, slice(0, 256), req1_ids)
    rows_out1 = send(out_rows.at[1], rows_in.at[1], other)
    rows_out1.start()
    src1_b = updated(src1, src1_st, slice(256, 512), src1_ids)
    src1[...] = src1_b.astype(F32)
    queries = product(src1[...], rel1[...])
    queries_row, queries_b = queries.T.astype(BF16), queries.astype(BF16)

    for tile in range(SHARE // GROUP):
        at = slice(tile * GROUP, (tile + 1) * GROUP)
        grads = summed(c0, 0, 0, tile_ids(tile)) + summed(c0, 1, 2, tile_ids(tile))
        rows = tab[:, pl.ds(pl.multiple_of(own_first + tile * GROUP, GROUP), GROUP)]
        own[:, at], own_st[0:1, at] = adagrad(rows, own_st[0:1, at], grads)

    rows_out1.wait_recv()
    backs1, shares1 = back_copies(1, c1, other, 1), share_copies(c1)
    coeffs = coefficients(queries_row, rows_in[1], live_s[1])
    d_queries = mat(rows_in[1], coeffs.T.astype(BF16))
    drel[1, :, 0:W] = conj_product(d_queries, src1[...]).T.astype(BF16)

    drel_sends[1].start()

    def quarter(ref, lo):
        return at_rows(ref, lo, FIRST_PART)

    my_lo = [lax.rem(first + k, 4) * FIRST_PART for k in (1, 2, 3, 0)]
    chains = range(CHAINS)
    firsts = [
        [
            send(at_rows(hsend, my_lo[k] + t * CHAIN, CHAIN), xin.at[k, pl.ds(t * CHAIN, CHAIN), :], first_peers[k])
            for k in range(3)
        ]
        for t in chains
    ]
    for lo in my_lo:
        quarter(h0, lo)[...] += relation_part(1, drel, msg[5:6, :], lo)
    drel_sends[1].wait_recv()
    for k in range(4):
        total = quarter(h0, my_lo[k])[...] + relation_part(1, dmate, comb[core_rep, 5:6, :], my_lo[k])
        if k < 3:
            quarter(hsend, my_lo[k])[...] = total.astype(BF16)
            firsts[0][k].start()
        else:
            qsum[...] = total
    start(firsts[1] + firsts[2])

    back[1] = mat(queries_b, coeffs.astype(BF16)).astype(BF16)
    start(backs1)
    c1[:, mine_at(0)] = conj_product(d_queries, rel1[...]).astype(BF16)
    for group in shares1[0]:
        start(group[:2])

    seconds = [
        [
            send(
                at_rows(qsend, t * CHAIN + lax.rem(second + k, 4) * THIRD_PART, THIRD_PART),
                sin.at[k - 1, pl.ds(t * THIRD_PART, THIRD_PART), :],
                second_peers[k - 1],
            )
            for k in range(1, 4)
        ]
        for t in chains
    ]
    for t in chains:
        at = slice(t * CHAIN, (t + 1) * CHAIN)
        total = qsum[at, :]
        for k in range(3):
            firsts[t][k].wait_recv()
            total = total + xin[k, at, :].astype(F32)
        qsum[at, :] = total
        qsend[at, :] = total.astype(BF16)
        start(seconds[t])

    thirds = [
        send(at_rows(rsend, third(k)[1] * THIRD_PART, THIRD_PART), zin.at[k - 1], z_peers[k - 1])
        for k in range(1, 8)
    ]
    for t in chains:
        at = slice(t * THIRD_PART, (t + 1) * THIRD_PART)
        total = at_rows(qsum, t * CHAIN + second * THIRD_PART, THIRD_PART)[...]
        for k in range(3):
            seconds[t][k].wait_recv()
            total = total + sin[k, at, :].astype(F32)
        rsum[at, :] = total
        rsend[at, :] = total.astype(BF16)
        for k in range(1, 8):
            pl.when(holds(k, t))(thirds[k - 1].start)

    for k in range(len(PIECES)):
        backs1[k].wait_recv()
        start(shares1[1][k][:2])
        shares1[0][k][1].wait_recv()
        shares1[0][k][2].start()

    third_rows = at_rows(dall, third_row, THIRD_PART)
    out_z = [send(third_rows, third_rows, device) for device in z_peers]

    @pl.when(sums_third)
    def _():
        total = at_rows(rsum, my_third * THIRD_PART, THIRD_PART)[...]
        for k in range(7):
            thirds[k].wait_recv()
            total = total + zin[k].astype(F32)
        mean = jnp.sum(total * total, axis=1, keepdims=True) * (1.0 / W)
        delta = -RATE * total / (jnp.sqrt(rst[:, 0:1] + mean) + EPS)
        mean_hi = mean.astype(BF16).astype(F32)
        lane = iota((THIRD_PART, WIDE), 1)
        delta = jnp.where(lane == W, mean_hi, jnp.where(lane == W + 1, mean - mean_hi, delta))
        third_rows[...] = delta.astype(BF16)
        start(out_z)

    for group in shares1[1]:
        group[1].wait_recv()
        group[2].start()
    for kind in range(2):
        for group in shares1[kind]:
            group[0].wait_recv()
            group[2].wait_recv()

    def own_tiles(tiles):
        for tile in tiles:
            at = slice(tile * GROUP, (tile + 1) * GROUP)
            grads = summed(c1, 0, 1, tile_ids(tile)) + summed(c1, 1, 3, tile_ids(tile))
            own[:, at], own_st[0:1, at] = adagrad(own[:, at], own_st[0:1, at], grads)

    own_tiles((0,))
    out_second, out_first, swaps = [], [], []
    for t in chains:
        for k in range(1, 8):
            pl.when(holds(-k, t))(out_z[k - 1].wait_recv)
        rows = at_rows(dall, first_row + t * CHAIN + second * THIRD_PART, THIRD_PART)
        out_second.append([send(rows, rows, device) for device in second_peers])
        start(out_second[t])
    own_tiles((1,))
    for t in chains:
        for copy in out_second[t]:
            copy.wait_recv()
        rows = at_rows(dall, first_row + t * CHAIN, CHAIN)
        out_first.append([send(rows, rows, device) for device in first_peers])
        start(out_first[t])
        swaps.append(send(rows, rows, core_mate))
        swaps[t].start()
    own_tiles((2, 3))
    for k in range(8):
        est_ref[k : k + 1, :] = own_st[0:1, k * 128 : (k + 1) * 128]
    for t in chains:
        for k in range(3):
            out_first[t][k].wait_recv()
            rows = at_rows(dall, mine_from + lax.rem(first + 3 - k, 4) * FIRST_PART + t * CHAIN, CHAIN)
            swaps.append(send(rows, rows, core_mate))
            swaps[-1].start()

    def turn(lo, size):
        rows = dall[lo : lo + HALF_SLOTS, :].astype(F32).T[:, 0:size]
        rtab[:, lo : lo + size] = rtab[:, lo : lo + size] + rows[0:W]
        mean_ref[0:1, lo : lo + size] = rows[W : W + 1] + rows[W + 1 : W + 2]

    halves = ((0, HALF_SLOTS), (HALF_SLOTS, RELS - HALF_SLOTS))
    for c in range(2):
        pl.when(core == c)(functools.partial(turn, *halves[c]))
    for copy in swaps:
        copy.wait_recv()
    for c in range(2):
        pl.when(core == c)(functools.partial(turn, *halves[1 - c]))

    for copy in [ask0, ask1, rows_out0, rows_out1] + combs + backs0 + backs0_y + backs1 + drel_sends:
        copy.wait_send()
    for group in shares0 + pass_on + shares1[0] + shares1[1]:
        for copy in group:
            copy.wait_send()
    for group in firsts + seconds + out_second + out_first + [swaps]:
        for copy in group:
            copy.wait_send()
    for k in range(1, 8):
        pl.when(third(k)[0])(thirds[k - 1].wait_send)

    @pl.when(sums_third)
    def _():
        for copy in out_z:
            copy.wait_send()


OWN_PIECES = ((0, 104), (104, 104), (208, 96), (304, 96))


def finish(own, own_state, relations, mean, rstate, ent_hbm, est_ref, rel_hbm, nstate, sem):
    stores = [
        pltpu.make_async_copy(source.at[pl.ds(lo, size), :], target.at[pl.ds(lo, size), :], sem.at[first + k])
        for source, target, first in ((own, ent_hbm, 0), (relations, rel_hbm, 4))
        for k, (lo, size) in enumerate(OWN_PIECES)
    ]
    for store in stores:
        store.start()
    est_ref[...] = own_state[...]
    nstate[...] = rstate[...] + mean[0:1, :].reshape(SLOTS)[:RELS]
    for store in stores:
        store.wait()


def per_device(
    entity_table, entity_state, relation_table, relation_state, source_rows, target_rows, relation_ids, live_counts
):
    vmem, ids = pl.BlockSpec(memory_space=pltpu.VMEM), pltpu.VMEM((2, 1, GROUP), I32)
    anywhere = pl.BlockSpec(memory_space=pl.ANY)
    contributions = pltpu.VMEM((W, 8 * GROUP), BF16)
    blocks = pltpu.VMEM((2, W, GROUP), BF16)
    block_f, state_row = pltpu.VMEM((W, GROUP), F32), pltpu.VMEM((8, GROUP), F32)
    own, own_state, new_relations, mean = pl.pallas_call(
        kernel,
        out_shape=(
            pltpu.VMEM((W, SHARE), F32),
            pltpu.VMEM((8, 128), F32),
            pltpu.VMEM((W, RELS), F32),
            pltpu.VMEM((8, SLOTS), F32),
        ),
        in_specs=[anywhere] * 8,
        out_specs=(vmem, vmem, vmem, vmem),
        scratch_shapes=[
            pltpu.VMEM((W, ROWS), F32),
            pltpu.VMEM((W + 16, ROWS), BF16),
            pltpu.VMEM((W, RELS), BF16),
            pltpu.VMEM((16, ROWS), F32),
            pltpu.VMEM((ROWS // 128, 128), F32),
            pltpu.SMEM((RELS,), F32),
            ids, ids, ids,
            pltpu.SMEM((2,), I32),
            pltpu.VMEM((8, GROUP), I32),
            pltpu.VMEM((2, 8, GROUP), I32),
            pltpu.VMEM((4, 8, GROUP), I32),
            pltpu.VMEM((4, 4 * GROUP, 1), F32),
            blocks, blocks, blocks,
            contributions, contributions,
            pltpu.VMEM((W, 2 * GROUP), F32),
            block_f, block_f, state_row, state_row, block_f,
            pltpu.VMEM((2, GROUP, WIDE), BF16),
            pltpu.VMEM((8, SHARE), F32),
            pltpu.VMEM((HALF_SLOTS, WIDE), F32),
            pltpu.VMEM((HALF_SLOTS, WIDE), BF16),
            pltpu.VMEM((2, GROUP, WIDE), BF16),
            pltpu.VMEM((3, FIRST_PART, WIDE), BF16),
            pltpu.VMEM((FIRST_PART, WIDE), F32),
            pltpu.VMEM((FIRST_PART, WIDE), BF16),
            pltpu.VMEM((3, CHAINS * THIRD_PART, WIDE), BF16),
            pltpu.VMEM((CHAINS * THIRD_PART, WIDE), F32),
            pltpu.VMEM((CHAINS * THIRD_PART, WIDE), BF16),
            pltpu.VMEM((7, THIRD_PART, WIDE), BF16),
            pltpu.VMEM((THIRD_PART, 128), F32),
            pltpu.VMEM((SLOTS, WIDE), BF16),
            pltpu.SemaphoreType.DMA((11,)),
            pltpu.SemaphoreType.DMA((SEMS,)),
            pltpu.SemaphoreType.DMA((SEMS,)),
        ],
        compiler_params=pltpu.CompilerParams(
            collective_id=0, has_side_effects=True, vmem_limit_bytes=58 * 1024 * 1024
        ),
    )(
        entity_table.T, relation_table.T, entity_state.reshape(ROWS // 128, 128), relation_state,
        source_rows, target_rows, relation_ids, live_counts.reshape(-1),
    )
    own, own_state, new_relations, new_state = pl.pallas_call(
        finish,
        out_shape=(
            jax.ShapeDtypeStruct((W, SHARE), F32),
            jax.ShapeDtypeStruct((8, 128), F32),
            jax.ShapeDtypeStruct((W, RELS), F32),
            jax.ShapeDtypeStruct((RELS,), F32),
        ),
        in_specs=[vmem, vmem, vmem, vmem, vmem],
        out_specs=(anywhere, vmem, anywhere, vmem),
        scratch_shapes=[
            pltpu.SemaphoreType.DMA((8,)),
        ],
        compiler_params=pltpu.CompilerParams(vmem_limit_bytes=12 * 1024 * 1024),
    )(own, own_state, new_relations, mean, relation_state)
    return own.T, own_state.reshape(-1), new_relations.T, new_state


def solution(mesh):
    in_specs = (
        P("dom", None),
        P("dom"),
        P(),
        P(),
        P(None, "dom", "rep"),
        P(None, "dom", "rep"),
        P(None, "dom", "rep"),
        P(None, "dom", "rep"),
    )
    out_specs = (P(("dom", "rep"), None), P(("dom", "rep")), P(), P())
    return jax.shard_map(per_device, mesh=mesh, in_specs=in_specs, out_specs=out_specs, check_vma=False)
```

```python
import functools

import jax
import jax.numpy as jnp
from jax import lax
from jax.experimental import pallas as pl
from jax.experimental.pallas import tpu as pltpu
from jax.sharding import PartitionSpec as P

MESH = pl.DeviceIdType.MESH
F32, BF16, I32 = jnp.float32, jnp.bfloat16, jnp.int32

RATE = 0.2
EPS = 1e-06
W = 400
HALF = 200
TALL = 416
WIDE = 512
ROWS = 4096
SHARE = 1024
GROUP = 256
RELS = 1300
HALF_SLOTS = 768
SLOTS = 2 * HALF_SLOTS
FIRST_PART, CHAIN, THIRD_PART = 192, 64, 16
CHAINS = 3
PIECES = ((0, 208), (208, 192))
SEMS = 128


def mat(a, b):
    return jnp.dot(a, b, preferred_element_type=F32)


def iota(shape, dim):
    return lax.broadcasted_iota(I32, shape, dim)


def indicator(hit):
    return jnp.where(hit, 1.0, 0.0).astype(BF16)


def columns(rows):
    eye = indicator(iota((GROUP, GROUP), 0) == iota((GROUP, GROUP), 1))

    def turned(part):
        return lax.dot_general(
            eye, part.astype(F32).astype(BF16), (((1,), (1,)), ((), ())), preferred_element_type=F32
        )

    return turned(lax.shift_right_logical(rows, 8)) * 256.0 + turned(jnp.bitwise_and(rows, 255))


def adagrad(rows, state, grads):
    state = state + jnp.sum(grads * grads, axis=0, keepdims=True) * (1.0 / W)
    return rows - RATE * grads / (jnp.sqrt(state) + EPS), state


def kernel(
    tab_hbm, rtab_hbm, state_hbm, rstate_hbm, src_hbm, tgt_hbm, rid_hbm, live_hbm,
    own, est_ref, rtab, mean_ref,
    tab, parts, rtab_b, st_parts, state_v, rstate_s, src_v, tgt_v, rid_v, live_s, msg, idx_in, comb, cid,
    out_rows, rows_in, back, c0, c1, gsum, req1, src1, req1_st, src1_st, rel1, drel, own_st,
    h0, hsend, dmate, xin, qsum, qsend, sin, rsum, rsend, zin, rst, dall,
    local_sem, send_sem, recv_sem,
):
    dom, rep = lax.axis_index("dom"), lax.axis_index("rep")
    core, y_lo = lax.rem(rep, 2), lax.div(rep, 2)
    x, z, y_hi = lax.rem(dom, 4), lax.rem(lax.div(dom, 4), 8), lax.div(dom, 32)
    y = 2 * y_hi + y_lo
    plane = 32 * y_hi

    core_rep, y_rep = rep + 1 - 2 * core, lax.rem(rep + 2, 4)
    core_mate, y_mate = (dom, core_rep), (dom, y_rep)
    cross_mate = (dom, y_rep + 1 - 2 * core)
    after = (lax.rem(dom + 1, 64), rep)
    before = (lax.rem(dom + 63, 64), rep)
    before_y, after_y = (lax.rem(dom + 63, 64), y_rep), (lax.rem(dom + 1, 64), y_rep)
    other = (lax.rem(dom + 32, 64), y_rep)
    opposite = (lax.rem(dom + 32, 64), rep)
    x_peers = [(plane + 4 * z + lax.rem(x + k, 4), rep) for k in range(1, 4)]
    z_peers = [(plane + 4 * lax.rem(z + k, 8) + x, rep) for k in range(1, 8)]

    def beside(in_x, in_y):
        y_there = lax.rem(y + in_y, 4)
        return 32 * lax.div(y_there, 2) + 4 * z + lax.rem(x + in_x, 4), 2 * lax.rem(y_there, 2) + core

    first_peers = [beside((1 - core) * k, core * k) for k in range(1, 4)]
    second_peers = [beside(core * k, (1 - core) * k) for k in range(1, 4)]
    first, second = (1 - core) * x + core * y, core * x + (1 - core) * y
    mine_from = core * HALF_SLOTS

    def third(k):
        place = lax.rem(z + 4 * core + k + 8, 8)
        return lax.rem(place, 3) == 0, lax.div(place, 3)

    def holds(k, t):
        return lax.rem(z + 4 * core + k + 8, 8) == 3 * t

    count = [0]

    def send(src, dst, device):
        i = count[0]
        count[0] += 1
        assert i < SEMS
        return pltpu.make_async_remote_copy(
            src_ref=src, dst_ref=dst, send_sem=send_sem.at[i], recv_sem=recv_sem.at[i],
            device_id=device, device_id_type=MESH,
        )

    def start(copies):
        for copy in copies:
            copy.start()

    def lanes(ref, lo, size):
        return ref.at[:, pl.ds(pl.multiple_of(lo, 128), size)]

    def at_rows(ref, lo, size):
        return ref.at[pl.ds(pl.multiple_of(lo, 16), size), :]

    loads = [
        pltpu.make_async_copy(lanes(tab_hbm, k * 1024, 1024), lanes(tab, k * 1024, 1024), local_sem.at[k])
        for k in range(4)
    ]
    smalls = [
        pltpu.make_async_copy(source, target, local_sem.at[5 + k])
        for k, (source, target) in enumerate(
            (
                (src_hbm, src_v), (tgt_hbm, tgt_v), (rid_hbm, rid_v), (live_hbm, live_s),
                (state_hbm, state_v), (rstate_hbm, rstate_s),
            )
        )
    ]
    start(smalls)
    start(loads)
    load_rtab = pltpu.make_async_copy(rtab_hbm, rtab, local_sem.at[4])

    barrier = pltpu.get_barrier_semaphore()
    greeted = [core_mate, y_mate, cross_mate, after, before, after_y, before_y, other, opposite] + x_peers + z_peers
    for device in greeted:
        pl.semaphore_signal(barrier, inc=1, device_id=device, device_id_type=MESH)
    for copy in smalls:
        copy.wait()
    for t in range(2):
        msg[t : t + 1, :] = src_v[t]
        msg[2 + t : 3 + t, :] = tgt_v[t]
        msg[4 + t : 5 + t, :] = rid_v[t]
    msg[6:8, :] = jnp.full((2, GROUP), live_s[0], I32)
    pl.semaphore_wait(barrier, len(greeted))

    ask0 = send(msg, idx_in.at[0], after)
    ask1 = send(msg, idx_in.at[1], other)
    start([ask0, ask1])

    def lookup(table, ids):
        return mat(table, indicator(iota((table.shape[1], GROUP), 0) == ids))

    st_parts[...] = jnp.zeros(st_parts.shape, F32)
    for k in range(ROWS // 128):
        whole = state_v[k : k + 1, :]
        top = whole.astype(BF16).astype(F32)
        mid = (whole - top).astype(BF16).astype(F32)
        st_parts[0:1, k * 128 : (k + 1) * 128] = top
        st_parts[1:2, k * 128 : (k + 1) * 128] = mid
        st_parts[2:3, k * 128 : (k + 1) * 128] = whole - top - mid
    parts[W : W + 16, :] = st_parts[...].astype(BF16)

    sums_third, my_third = third(0)
    first_row = mine_from + first * FIRST_PART
    third_row = pl.multiple_of(first_row + my_third * CHAIN + second * THIRD_PART, 16)
    for k in range(THIRD_PART):
        rst[k : k + 1, :] = jnp.full((1, 128), rstate_s[jnp.minimum(third_row + k, RELS - 1)], F32)
    for k in range(8):
        own_st[0:1, k * 128 : (k + 1) * 128] = state_v[pl.ds(rep * 8 + k, 1), :]

    drel[...] = jnp.zeros(drel.shape, BF16)

    def high(k, carry):
        at = pl.ds(pl.multiple_of(k * 256, 256), 256)
        parts[0:W, at] = tab[:, at].astype(BF16)
        return carry

    for k in range(4):
        loads[k].wait()
        lax.fori_loop(4 * k, 4 * k + 4, high, 0)
    load_rtab.start()

    out_rows[0] = lookup(parts[0:W, :], msg[0:1, :]).astype(BF16)
    rows_out0 = send(out_rows.at[0], rows_in.at[0], after)
    rows_out0.start()

    def product(a, b):
        return jnp.concatenate(
            [a[:HALF] * b[:HALF] - a[HALF:] * b[HALF:], a[:HALF] * b[HALF:] + a[HALF:] * b[:HALF]], axis=0
        )

    def conj_product(a, b):
        return jnp.concatenate(
            [a[:HALF] * b[:HALF] + a[HALF:] * b[HALF:], a[HALF:] * b[:HALF] - a[:HALF] * b[HALF:]], axis=0
        )

    def coefficients(queries_row, tgt, live):
        scores = mat(queries_row, tgt)
        row_id, col_id = iota((GROUP, GROUP), 0), iota((GROUP, GROUP), 1)
        terms = jnp.where(col_id < live, jnp.exp(scores), 0.0)
        probs = terms / jnp.sum(terms, axis=1, keepdims=True)
        return jnp.where(row_id < live, probs - jnp.where(row_id == col_id, 1.0, 0.0), 0.0)

    def block_at(ref, holder, kind, piece):
        lo, size = PIECES[piece]
        return ref.at[pl.ds(lo, size), pl.ds(pl.multiple_of(kind * 1024 + holder * GROUP, GROUP), GROUP)]

    def share_in_rep(ref, kind, piece):
        mine, got = block_at(ref, rep, kind, piece), block_at(ref, y_rep, kind, piece)
        return send(mine, mine, core_mate), send(mine, mine, y_mate), send(got, got, core_mate)

    def back_copies(t, ref, to, kind):
        return [
            send(back.at[t, pl.ds(lo, size), :], block_at(ref, to[1], kind, k), to)
            for k, (lo, size) in enumerate(PIECES)
        ]

    def share_copies(ref):
        return [[share_in_rep(ref, kind, k) for k in range(len(PIECES))] for kind in range(2)]

    def mine_at(kind):
        return pl.ds(pl.multiple_of(kind * 1024 + rep * GROUP, GROUP), GROUP)

    ask0.wait_recv()
    ask1.wait_recv()
    comb[rep, 0:2, :] = msg[0:2, :]
    comb[rep, 2:3, :] = idx_in[0, 2:3, :]
    comb[rep, 3:4, :] = idx_in[1, 3:4, :]
    comb[rep, 4:5, :] = idx_in[0, 4:5, :]
    comb[rep, 5:6, :] = msg[5:6, :]
    comb[rep, 6:8, :] = jnp.zeros((2, GROUP), I32)
    combs = [send(comb.at[rep], comb.at[rep], device) for device in (core_mate, y_mate, cross_mate)]
    start(combs)

    tgt0 = lookup(parts[0:W, :], idx_in[0, 2:3, :]).astype(BF16)
    load_rtab.wait()
    rtab_b[...] = rtab[...].astype(BF16)
    rel0 = lookup(rtab_b[...], idx_in[0, 4:5, :])

    def lookup_all(ids, rows, state):
        got = lookup(parts[...], ids)
        state[0:1, :] = got[W : W + 1] + got[W + 1 : W + 2] + got[W + 2 : W + 3]
        rows[...] = got[0:W]

    req1_ids, src1_ids = idx_in[1, 3:4, :], msg[1:2, :]
    lookup_all(req1_ids, req1, req1_st)

    backs0, shares0 = back_copies(0, c0, before, 0), share_copies(c0)[1]
    backs0_y = [
        send(back.at[0, pl.ds(lo, size), :], block_at(c0, rep, 0, k), before_y)
        for k, (lo, size) in enumerate(PIECES)
    ]
    pass_on = [
        [send(block_at(c0, holder, 0, k), block_at(c0, holder, 0, k), core_mate) for holder in (rep, y_rep)]
        for k in range(len(PIECES))
    ]
    rows_out0.wait_recv()
    src0 = rows_in[0].astype(F32)
    queries = product(src0, rel0)
    coeffs = coefficients(queries.T.astype(BF16), tgt0, idx_in[0, 6:7, :])
    d_queries = mat(tgt0, coeffs.T.astype(BF16))
    back[0] = conj_product(d_queries, rel0).astype(BF16)
    for k in range(len(PIECES)):
        backs0[k].start()
        backs0_y[k].start()
    c0[:, mine_at(1)] = mat(queries.astype(BF16), coeffs.astype(BF16)).astype(BF16)
    for group in shares0:
        start(group[:2])
    drel[0, :, 0:W] = conj_product(d_queries, src0).T.astype(BF16)
    drel_sends = [send(drel.at[t], dmate.at[t], core_mate) for t in range(2)]
    drel_sends[0].start()

    lookup_all(src1_ids, src1, src1_st)
    for copy in combs:
        copy.wait_recv()
    for b in range(4):
        turned = columns(comb[b])
        for q in range(4):
            cid[q, b * GROUP : (b + 1) * GROUP, :] = turned[:, q : q + 1]
    for k in range(len(PIECES)):
        shares0[k][1].wait_recv()
        shares0[k][2].start()

    for group in shares0:
        group[0].wait_recv()
        group[2].wait_recv()

    def summed(ref, kind, q, ids):
        return mat(ref[:, kind * 1024 : (kind + 1) * 1024], indicator(cid[q] == ids.astype(F32)))

    own_first = rep * SHARE

    def tile_ids(tile):
        return iota((1, GROUP), 1) + (own_first + tile * GROUP)

    gsum[:, 0:256] = summed(c0, 1, 2, req1_ids)
    gsum[:, 256:512] = summed(c0, 1, 2, src1_ids)

    def relation_part(t, rows, rid, lo):
        ids = iota((FIRST_PART, 1), 0) + (mine_from + lo)
        return mat(indicator(ids == rid), rows[t])

    drel_sends[0].wait_recv()
    for lo in range(0, HALF_SLOTS, FIRST_PART):
        h0[lo : lo + FIRST_PART, :] = relation_part(0, drel, idx_in[0, 4:5, :], lo) + relation_part(
            0, dmate, comb[core_rep, 4:5, :], lo
        )
    rel1[...] = lookup(rtab_b[...], msg[5:6, :])
    for k in range(len(PIECES)):
        backs0[k].wait_recv()
        pass_on[k][0].start()
        backs0_y[k].wait_recv()
        pass_on[k][1].start()

    for group in pass_on:
        for copy in group:
            copy.wait_recv()

    def updated(rows, state, at, ids):
        grads = gsum[:, at] + summed(c0, 0, 0, ids)
        return adagrad(rows[...], state[0:1, :], grads)[0].astype(BF16)

    out_rows[1] = updated(req1, req1_st, slice(0, 256), req1_ids)
    rows_out1 = send(out_rows.at[1], rows_in.at[1], other)
    rows_out1.start()
    src1_b = updated(src1, src1_st, slice(256, 512), src1_ids)
    src1[...] = src1_b.astype(F32)
    queries = product(src1[...], rel1[...])
    queries_row, queries_b = queries.T.astype(BF16), queries.astype(BF16)

    for tile in range(SHARE // GROUP):
        at = slice(tile * GROUP, (tile + 1) * GROUP)
        grads = summed(c0, 0, 0, tile_ids(tile)) + summed(c0, 1, 2, tile_ids(tile))
        rows = tab[:, pl.ds(pl.multiple_of(own_first + tile * GROUP, GROUP), GROUP)]
        own[:, at], own_st[0:1, at] = adagrad(rows, own_st[0:1, at], grads)

    rows_out1.wait_recv()
    backs1, shares1 = back_copies(1, c1, other, 1), share_copies(c1)
    coeffs = coefficients(queries_row, rows_in[1], live_s[1])
    d_queries = mat(rows_in[1], coeffs.T.astype(BF16))
    drel[1, :, 0:W] = conj_product(d_queries, src1[...]).T.astype(BF16)

    drel_sends[1].start()

    def quarter(ref, lo):
        return at_rows(ref, lo, FIRST_PART)

    my_lo = [lax.rem(first + k, 4) * FIRST_PART for k in (1, 2, 3, 0)]
    chains = range(CHAINS)
    firsts = [
        [
            send(at_rows(hsend, my_lo[k] + t * CHAIN, CHAIN), xin.at[k, pl.ds(t * CHAIN, CHAIN), :], first_peers[k])
            for k in range(3)
        ]
        for t in chains
    ]
    for lo in my_lo:
        quarter(h0, lo)[...] += relation_part(1, drel, msg[5:6, :], lo)
    drel_sends[1].wait_recv()
    for k in range(4):
        total = quarter(h0, my_lo[k])[...] + relation_part(1, dmate, comb[core_rep, 5:6, :], my_lo[k])
        if k < 3:
            quarter(hsend, my_lo[k])[...] = total.astype(BF16)
            firsts[0][k].start()
        else:
            qsum[...] = total
    start(firsts[1] + firsts[2])

    back[1] = mat(queries_b, coeffs.astype(BF16)).astype(BF16)
    c1[:, mine_at(0)] = conj_product(d_queries, rel1[...]).astype(BF16)

    seconds = [
        [
            send(
                at_rows(qsend, t * CHAIN + lax.rem(second + k, 4) * THIRD_PART, THIRD_PART),
                sin.at[k - 1, pl.ds(t * THIRD_PART, THIRD_PART), :],
                second_peers[k - 1],
            )
            for k in range(1, 4)
        ]
        for t in chains
    ]
    for t in chains:
        at = slice(t * CHAIN, (t + 1) * CHAIN)
        total = qsum[at, :]
        for k in range(3):
            firsts[t][k].wait_recv()
            total = total + xin[k, at, :].astype(F32)
        qsum[at, :] = total
        qsend[at, :] = total.astype(BF16)
        start(seconds[t])
    start(backs1)
    for group in shares1[0]:
        start(group[:2])

    thirds = [
        send(at_rows(rsend, third(k)[1] * THIRD_PART, THIRD_PART), zin.at[k - 1], z_peers[k - 1])
        for k in range(1, 8)
    ]
    for t in chains:
        at = slice(t * THIRD_PART, (t + 1) * THIRD_PART)
        total = at_rows(qsum, t * CHAIN + second * THIRD_PART, THIRD_PART)[...]
        for k in range(3):
            seconds[t][k].wait_recv()
            total = total + sin[k, at, :].astype(F32)
        rsum[at, :] = total
        rsend[at, :] = total.astype(BF16)
        for k in range(1, 8):
            pl.when(holds(k, t))(thirds[k - 1].start)

    third_rows = at_rows(dall, third_row, THIRD_PART)
    out_z = [send(third_rows, third_rows, device) for device in z_peers]

    @pl.when(sums_third)
    def _():
        total = at_rows(rsum, my_third * THIRD_PART, THIRD_PART)[...]
        for k in range(7):
            thirds[k].wait_recv()
            total = total + zin[k].astype(F32)
        mean = jnp.sum(total * total, axis=1, keepdims=True) * (1.0 / W)
        delta = -RATE * total / (jnp.sqrt(rst[:, 0:1] + mean) + EPS)
        mean_hi = mean.astype(BF16).astype(F32)
        lane = iota((THIRD_PART, WIDE), 1)
        delta = jnp.where(lane == W, mean_hi, jnp.where(lane == W + 1, mean - mean_hi, delta))
        third_rows[...] = delta.astype(BF16)
        start(out_z)

    for k in range(len(PIECES)):
        backs1[k].wait_recv()
        start(shares1[1][k][:2])
        shares1[0][k][1].wait_recv()
        shares1[0][k][2].start()
    def own_tiles(tiles):
        for tile in tiles:
            at = slice(tile * GROUP, (tile + 1) * GROUP)
            grads = summed(c1, 0, 1, tile_ids(tile)) + summed(c1, 1, 3, tile_ids(tile))
            own[:, at], own_st[0:1, at] = adagrad(own[:, at], own_st[0:1, at], grads)

    out_second, out_first, swaps = [], [], []
    for t in chains:
        for k in range(1, 8):
            pl.when(holds(-k, t))(out_z[k - 1].wait_recv)
        rows = at_rows(dall, first_row + t * CHAIN + second * THIRD_PART, THIRD_PART)
        out_second.append([send(rows, rows, device) for device in second_peers])
        start(out_second[t])
    for group in shares1[1]:
        group[1].wait_recv()
        group[2].start()
    for t in chains:
        for copy in out_second[t]:
            copy.wait_recv()
        rows = at_rows(dall, first_row + t * CHAIN, CHAIN)
        out_first.append([send(rows, rows, device) for device in first_peers])
        start(out_first[t])
        swaps.append(send(rows, rows, core_mate))
        swaps[t].start()
    for kind in range(2):
        for group in shares1[kind]:
            group[0].wait_recv()
            group[2].wait_recv()
    own_tiles((0, 1, 2, 3))
    for k in range(8):
        est_ref[k : k + 1, :] = own_st[0:1, k * 128 : (k + 1) * 128]
    for t in chains:
        for k in range(3):
            out_first[t][k].wait_recv()
            rows = at_rows(dall, mine_from + lax.rem(first + 3 - k, 4) * FIRST_PART + t * CHAIN, CHAIN)
            swaps.append(send(rows, rows, core_mate))
            swaps[-1].start()

    def turn(lo, size):
        rows = dall[lo : lo + HALF_SLOTS, :].astype(F32).T[:, 0:size]
        rtab[:, lo : lo + size] = rtab[:, lo : lo + size] + rows[0:W]
        mean_ref[0:1, lo : lo + size] = rows[W : W + 1] + rows[W + 1 : W + 2]

    halves = ((0, HALF_SLOTS), (HALF_SLOTS, RELS - HALF_SLOTS))
    for c in range(2):
        pl.when(core == c)(functools.partial(turn, *halves[c]))
    for copy in swaps:
        copy.wait_recv()
    for c in range(2):
        pl.when(core == c)(functools.partial(turn, *halves[1 - c]))

    for copy in [ask0, ask1, rows_out0, rows_out1] + combs + backs0 + backs0_y + backs1 + drel_sends:
        copy.wait_send()
    for group in shares0 + pass_on + shares1[0] + shares1[1]:
        for copy in group:
            copy.wait_send()
    for group in firsts + seconds + out_second + out_first + [swaps]:
        for copy in group:
            copy.wait_send()
    for k in range(1, 8):
        pl.when(third(k)[0])(thirds[k - 1].wait_send)

    @pl.when(sums_third)
    def _():
        for copy in out_z:
            copy.wait_send()


OWN_PIECES = ((0, 104), (104, 104), (208, 96), (304, 96))


def finish(own, own_state, relations, mean, rstate, ent_hbm, est_ref, rel_hbm, nstate, sem):
    stores = [
        pltpu.make_async_copy(source.at[pl.ds(lo, size), :], target.at[pl.ds(lo, size), :], sem.at[first + k])
        for source, target, first in ((own, ent_hbm, 0), (relations, rel_hbm, 4))
        for k, (lo, size) in enumerate(OWN_PIECES)
    ]
    for store in stores:
        store.start()
    est_ref[...] = own_state[...]
    nstate[...] = rstate[...] + mean[0:1, :].reshape(SLOTS)[:RELS]
    for store in stores:
        store.wait()


def per_device(
    entity_table, entity_state, relation_table, relation_state, source_rows, target_rows, relation_ids, live_counts
):
    vmem, ids = pl.BlockSpec(memory_space=pltpu.VMEM), pltpu.VMEM((2, 1, GROUP), I32)
    anywhere = pl.BlockSpec(memory_space=pl.ANY)
    contributions = pltpu.VMEM((W, 8 * GROUP), BF16)
    blocks = pltpu.VMEM((2, W, GROUP), BF16)
    block_f, state_row = pltpu.VMEM((W, GROUP), F32), pltpu.VMEM((8, GROUP), F32)
    own, own_state, new_relations, mean = pl.pallas_call(
        kernel,
        out_shape=(
            pltpu.VMEM((W, SHARE), F32),
            pltpu.VMEM((8, 128), F32),
            pltpu.VMEM((W, RELS), F32),
            pltpu.VMEM((8, SLOTS), F32),
        ),
        in_specs=[anywhere] * 8,
        out_specs=(vmem, vmem, vmem, vmem),
        scratch_shapes=[
            pltpu.VMEM((W, ROWS), F32),
            pltpu.VMEM((W + 16, ROWS), BF16),
            pltpu.VMEM((W, RELS), BF16),
            pltpu.VMEM((16, ROWS), F32),
            pltpu.VMEM((ROWS // 128, 128), F32),
            pltpu.SMEM((RELS,), F32),
            ids, ids, ids,
            pltpu.SMEM((2,), I32),
            pltpu.VMEM((8, GROUP), I32),
            pltpu.VMEM((2, 8, GROUP), I32),
            pltpu.VMEM((4, 8, GROUP), I32),
            pltpu.VMEM((4, 4 * GROUP, 1), F32),
            blocks, blocks, blocks,
            contributions, contributions,
            pltpu.VMEM((W, 2 * GROUP), F32),
            block_f, block_f, state_row, state_row, block_f,
            pltpu.VMEM((2, GROUP, WIDE), BF16),
            pltpu.VMEM((8, SHARE), F32),
            pltpu.VMEM((HALF_SLOTS, WIDE), F32),
            pltpu.VMEM((HALF_SLOTS, WIDE), BF16),
            pltpu.VMEM((2, GROUP, WIDE), BF16),
            pltpu.VMEM((3, FIRST_PART, WIDE), BF16),
            pltpu.VMEM((FIRST_PART, WIDE), F32),
            pltpu.VMEM((FIRST_PART, WIDE), BF16),
            pltpu.VMEM((3, CHAINS * THIRD_PART, WIDE), BF16),
            pltpu.VMEM((CHAINS * THIRD_PART, WIDE), F32),
            pltpu.VMEM((CHAINS * THIRD_PART, WIDE), BF16),
            pltpu.VMEM((7, THIRD_PART, WIDE), BF16),
            pltpu.VMEM((THIRD_PART, 128), F32),
            pltpu.VMEM((SLOTS, WIDE), BF16),
            pltpu.SemaphoreType.DMA((11,)),
            pltpu.SemaphoreType.DMA((SEMS,)),
            pltpu.SemaphoreType.DMA((SEMS,)),
        ],
        compiler_params=pltpu.CompilerParams(
            collective_id=0, has_side_effects=True, vmem_limit_bytes=58 * 1024 * 1024
        ),
    )(
        entity_table.T, relation_table.T, entity_state.reshape(ROWS // 128, 128), relation_state,
        source_rows, target_rows, relation_ids, live_counts.reshape(-1),
    )
    own, own_state, new_relations, new_state = pl.pallas_call(
        finish,
        out_shape=(
            jax.ShapeDtypeStruct((W, SHARE), F32),
            jax.ShapeDtypeStruct((8, 128), F32),
            jax.ShapeDtypeStruct((W, RELS), F32),
            jax.ShapeDtypeStruct((RELS,), F32),
        ),
        in_specs=[vmem, vmem, vmem, vmem, vmem],
        out_specs=(anywhere, vmem, anywhere, vmem),
        scratch_shapes=[
            pltpu.SemaphoreType.DMA((8,)),
        ],
        compiler_params=pltpu.CompilerParams(vmem_limit_bytes=12 * 1024 * 1024),
    )(own, own_state, new_relations, mean, relation_state)
    return own.T, own_state.reshape(-1), new_relations.T, new_state


def solution(mesh):
    in_specs = (
        P("dom", None),
        P("dom"),
        P(),
        P(),
        P(None, "dom", "rep"),
        P(None, "dom", "rep"),
        P(None, "dom", "rep"),
        P(None, "dom", "rep"),
    )
    out_specs = (P(("dom", "rep"), None), P(("dom", "rep")), P(), P())
    return jax.shard_map(per_device, mesh=mesh, in_specs=in_specs, out_specs=out_specs, check_vma=False)
```

```python
import functools

import jax
import jax.numpy as jnp
from jax import lax
from jax.experimental import pallas as pl
from jax.experimental.pallas import tpu as pltpu
from jax.sharding import PartitionSpec as P

MESH = pl.DeviceIdType.MESH
F32, BF16, I32 = jnp.float32, jnp.bfloat16, jnp.int32

RATE = 0.2
EPS = 1e-06
W = 400
HALF = 200
TALL = 416
WIDE = 512
ROWS = 4096
SHARE = 1024
GROUP = 256
RELS = 1300
HALF_SLOTS = 768
SLOTS = 2 * HALF_SLOTS
FIRST_PART, CHAIN, THIRD_PART = 192, 64, 16
CHAINS = 3
PIECES = ((0, 208), (208, 192))
SEMS = 128


def mat(a, b):
    return jnp.dot(a, b, preferred_element_type=F32)


def iota(shape, dim):
    return lax.broadcasted_iota(I32, shape, dim)


def indicator(hit):
    return jnp.where(hit, 1.0, 0.0).astype(BF16)


def columns(rows):
    eye = indicator(iota((GROUP, GROUP), 0) == iota((GROUP, GROUP), 1))

    def turned(part):
        return lax.dot_general(
            eye, part.astype(F32).astype(BF16), (((1,), (1,)), ((), ())), preferred_element_type=F32
        )

    return turned(lax.shift_right_logical(rows, 8)) * 256.0 + turned(jnp.bitwise_and(rows, 255))


def adagrad(rows, state, grads):
    state = state + jnp.sum(grads * grads, axis=0, keepdims=True) * (1.0 / W)
    return rows - RATE * grads / (jnp.sqrt(state) + EPS), state


def kernel(
    tab_hbm, rtab_hbm, state_hbm, rstate_hbm, src_hbm, tgt_hbm, rid_hbm, live_hbm,
    own, est_ref, rtab, mean_ref,
    tab, parts, rtab_b, st_parts, state_v, rstate_s, src_v, tgt_v, rid_v, live_s, msg, idx_in, comb, cid,
    out_rows, rows_in, back, c0, c1, gsum, req1, src1, req1_st, src1_st, rel1, drel, own_st,
    h0, hsend, dmate, xin, qsum, qsend, sin, rsum, rsend, zin, rst, dall,
    local_sem, send_sem, recv_sem,
):
    dom, rep = lax.axis_index("dom"), lax.axis_index("rep")
    core, y_lo = lax.rem(rep, 2), lax.div(rep, 2)
    x, z, y_hi = lax.rem(dom, 4), lax.rem(lax.div(dom, 4), 8), lax.div(dom, 32)
    y = 2 * y_hi + y_lo
    plane = 32 * y_hi

    core_rep, y_rep = rep + 1 - 2 * core, lax.rem(rep + 2, 4)
    core_mate, y_mate = (dom, core_rep), (dom, y_rep)
    cross_mate = (dom, y_rep + 1 - 2 * core)
    after = (lax.rem(dom + 1, 64), rep)
    before = (lax.rem(dom + 63, 64), rep)
    before_y, after_y = (lax.rem(dom + 63, 64), y_rep), (lax.rem(dom + 1, 64), y_rep)
    other = (lax.rem(dom + 32, 64), y_rep)
    opposite = (lax.rem(dom + 32, 64), rep)
    x_peers = [(plane + 4 * z + lax.rem(x + k, 4), rep) for k in range(1, 4)]
    z_peers = [(plane + 4 * lax.rem(z + k, 8) + x, rep) for k in range(1, 8)]

    def beside(in_x, in_y):
        y_there = lax.rem(y + in_y, 4)
        return 32 * lax.div(y_there, 2) + 4 * z + lax.rem(x + in_x, 4), 2 * lax.rem(y_there, 2) + core

    first_peers = [beside((1 - core) * k, core * k) for k in range(1, 4)]
    second_peers = [beside(core * k, (1 - core) * k) for k in range(1, 4)]
    first, second = (1 - core) * x + core * y, core * x + (1 - core) * y
    mine_from = core * HALF_SLOTS

    def third(k):
        place = lax.rem(z + 4 * core + k + 8, 8)
        return lax.rem(place, 3) == 0, lax.div(place, 3)

    def holds(k, t):
        return lax.rem(z + 4 * core + k + 8, 8) == 3 * t

    count = [0]

    def send(src, dst, device):
        i = count[0]
        count[0] += 1
        assert i < SEMS
        return pltpu.make_async_remote_copy(
            src_ref=src, dst_ref=dst, send_sem=send_sem.at[i], recv_sem=recv_sem.at[i],
            device_id=device, device_id_type=MESH,
        )

    def start(copies):
        for copy in copies:
            copy.start()

    def lanes(ref, lo, size):
        return ref.at[:, pl.ds(pl.multiple_of(lo, 128), size)]

    def at_rows(ref, lo, size):
        return ref.at[pl.ds(pl.multiple_of(lo, 16), size), :]

    loads = [
        pltpu.make_async_copy(lanes(tab_hbm, k * 1024, 1024), lanes(tab, k * 1024, 1024), local_sem.at[k])
        for k in range(4)
    ]
    smalls = [
        pltpu.make_async_copy(source, target, local_sem.at[5 + k])
        for k, (source, target) in enumerate(
            (
                (src_hbm, src_v), (tgt_hbm, tgt_v), (rid_hbm, rid_v), (live_hbm, live_s),
                (state_hbm, state_v), (rstate_hbm, rstate_s),
            )
        )
    ]
    start(smalls)
    start(loads)
    load_rtab = pltpu.make_async_copy(rtab_hbm, rtab, local_sem.at[4])

    barrier = pltpu.get_barrier_semaphore()
    greeted = [core_mate, y_mate, cross_mate, after, before, after_y, before_y, other, opposite] + x_peers + z_peers
    for device in greeted:
        pl.semaphore_signal(barrier, inc=1, device_id=device, device_id_type=MESH)
    for copy in smalls:
        copy.wait()
    for t in range(2):
        msg[t : t + 1, :] = src_v[t]
        msg[2 + t : 3 + t, :] = tgt_v[t]
        msg[4 + t : 5 + t, :] = rid_v[t]
    msg[6:8, :] = jnp.full((2, GROUP), live_s[0], I32)
    pl.semaphore_wait(barrier, len(greeted))

    ask0 = send(msg, idx_in.at[0], after)
    ask1 = send(msg, idx_in.at[1], other)
    start([ask0, ask1])

    def lookup(table, ids):
        return mat(table, indicator(iota((table.shape[1], GROUP), 0) == ids))

    st_parts[...] = jnp.zeros(st_parts.shape, F32)
    for k in range(ROWS // 128):
        whole = state_v[k : k + 1, :]
        top = whole.astype(BF16).astype(F32)
        mid = (whole - top).astype(BF16).astype(F32)
        st_parts[0:1, k * 128 : (k + 1) * 128] = top
        st_parts[1:2, k * 128 : (k + 1) * 128] = mid
        st_parts[2:3, k * 128 : (k + 1) * 128] = whole - top - mid
    parts[W : W + 16, :] = st_parts[...].astype(BF16)

    sums_third, my_third = third(0)
    first_row = mine_from + first * FIRST_PART
    third_row = pl.multiple_of(first_row + my_third * CHAIN + second * THIRD_PART, 16)
    for k in range(THIRD_PART):
        rst[k : k + 1, :] = jnp.full((1, 128), rstate_s[jnp.minimum(third_row + k, RELS - 1)], F32)
    for k in range(8):
        own_st[0:1, k * 128 : (k + 1) * 128] = state_v[pl.ds(rep * 8 + k, 1), :]

    drel[...] = jnp.zeros(drel.shape, BF16)

    def high(k, carry):
        at = pl.ds(pl.multiple_of(k * 256, 256), 256)
        parts[0:W, at] = tab[:, at].astype(BF16)
        return carry

    for k in range(4):
        loads[k].wait()
        lax.fori_loop(4 * k, 4 * k + 4, high, 0)
    load_rtab.start()

    out_rows[0] = lookup(parts[0:W, :], msg[0:1, :]).astype(BF16)
    rows_out0 = send(out_rows.at[0], rows_in.at[0], after)
    rows_out0.start()

    def product(a, b):
        return jnp.concatenate(
            [a[:HALF] * b[:HALF] - a[HALF:] * b[HALF:], a[:HALF] * b[HALF:] + a[HALF:] * b[:HALF]], axis=0
        )

    def conj_product(a, b):
        return jnp.concatenate(
            [a[:HALF] * b[:HALF] + a[HALF:] * b[HALF:], a[HALF:] * b[:HALF] - a[:HALF] * b[HALF:]], axis=0
        )

    def coefficients(queries_row, tgt, live):
        scores = mat(queries_row, tgt)
        row_id, col_id = iota((GROUP, GROUP), 0), iota((GROUP, GROUP), 1)
        terms = jnp.where(col_id < live, jnp.exp(scores), 0.0)
        probs = terms / jnp.sum(terms, axis=1, keepdims=True)
        return jnp.where(row_id < live, probs - jnp.where(row_id == col_id, 1.0, 0.0), 0.0)

    def block_at(ref, holder, kind, piece):
        lo, size = PIECES[piece]
        return ref.at[pl.ds(lo, size), pl.ds(pl.multiple_of(kind * 1024 + holder * GROUP, GROUP), GROUP)]

    def share_in_rep(ref, kind, piece):
        mine, got = block_at(ref, rep, kind, piece), block_at(ref, y_rep, kind, piece)
        return send(mine, mine, core_mate), send(mine, mine, y_mate), send(got, got, core_mate)

    def back_copies(t, ref, to, kind):
        return [
            send(back.at[t, pl.ds(lo, size), :], block_at(ref, to[1], kind, k), to)
            for k, (lo, size) in enumerate(PIECES)
        ]

    def share_copies(ref):
        return [[share_in_rep(ref, kind, k) for k in range(len(PIECES))] for kind in range(2)]

    def mine_at(kind):
        return pl.ds(pl.multiple_of(kind * 1024 + rep * GROUP, GROUP), GROUP)

    ask0.wait_recv()
    ask1.wait_recv()
    comb[rep, 0:2, :] = msg[0:2, :]
    comb[rep, 2:3, :] = idx_in[0, 2:3, :]
    comb[rep, 3:4, :] = idx_in[1, 3:4, :]
    comb[rep, 4:5, :] = idx_in[0, 4:5, :]
    comb[rep, 5:6, :] = msg[5:6, :]
    comb[rep, 6:8, :] = jnp.zeros((2, GROUP), I32)
    combs = [send(comb.at[rep], comb.at[rep], device) for device in (core_mate, y_mate, cross_mate)]
    start(combs)

    tgt0 = lookup(parts[0:W, :], idx_in[0, 2:3, :]).astype(BF16)
    load_rtab.wait()
    rtab_b[...] = rtab[...].astype(BF16)
    rel0 = lookup(rtab_b[...], idx_in[0, 4:5, :])

    def lookup_all(ids, rows, state):
        got = lookup(parts[...], ids)
        state[0:1, :] = got[W : W + 1] + got[W + 1 : W + 2] + got[W + 2 : W + 3]
        rows[...] = got[0:W]

    req1_ids, src1_ids = idx_in[1, 3:4, :], msg[1:2, :]
    lookup_all(req1_ids, req1, req1_st)

    backs0, shares0 = back_copies(0, c0, before, 0), share_copies(c0)[1]
    backs0_y = [
        send(back.at[0, pl.ds(lo, size), :], block_at(c0, rep, 0, k), before_y)
        for k, (lo, size) in enumerate(PIECES)
    ]
    pass_on = [
        [send(block_at(c0, holder, 0, k), block_at(c0, holder, 0, k), core_mate) for holder in (rep, y_rep)]
        for k in range(len(PIECES))
    ]
    rows_out0.wait_recv()
    src0 = rows_in[0].astype(F32)
    queries = product(src0, rel0)
    coeffs = coefficients(queries.T.astype(BF16), tgt0, idx_in[0, 6:7, :])
    d_queries = mat(tgt0, coeffs.T.astype(BF16))
    back[0] = conj_product(d_queries, rel0).astype(BF16)
    for k in range(len(PIECES)):
        backs0[k].start()
        backs0_y[k].start()
    c0[:, mine_at(1)] = mat(queries.astype(BF16), coeffs.astype(BF16)).astype(BF16)
    for group in shares0:
        start(group[:2])
    drel[0, :, 0:W] = conj_product(d_queries, src0).T.astype(BF16)
    drel_sends = [send(drel.at[t], dmate.at[t], core_mate) for t in range(2)]
    drel_sends[0].start()

    lookup_all(src1_ids, src1, src1_st)
    for copy in combs:
        copy.wait_recv()
    for b in range(4):
        turned = columns(comb[b])
        for q in range(4):
            cid[q, b * GROUP : (b + 1) * GROUP, :] = turned[:, q : q + 1]
    def relation_part(t, rows, rid, lo):
        ids = iota((FIRST_PART, 1), 0) + (mine_from + lo)
        return mat(indicator(ids == rid), rows[t])

    drel_sends[0].wait_recv()
    for lo in range(0, HALF_SLOTS, FIRST_PART):
        h0[lo : lo + FIRST_PART, :] = relation_part(0, drel, idx_in[0, 4:5, :], lo) + relation_part(
            0, dmate, comb[core_rep, 4:5, :], lo
        )
    rel1[...] = lookup(rtab_b[...], msg[5:6, :])

    for k in range(len(PIECES)):
        shares0[k][1].wait_recv()
        shares0[k][2].start()
        backs0[k].wait_recv()
        pass_on[k][0].start()
        backs0_y[k].wait_recv()
        pass_on[k][1].start()
    for group in shares0:
        group[0].wait_recv()
        group[2].wait_recv()

    def summed(ref, kind, q, ids):
        return mat(ref[:, kind * 1024 : (kind + 1) * 1024], indicator(cid[q] == ids.astype(F32)))

    own_first = rep * SHARE

    def tile_ids(tile):
        return iota((1, GROUP), 1) + (own_first + tile * GROUP)

    gsum[:, 0:256] = summed(c0, 1, 2, req1_ids)
    gsum[:, 256:512] = summed(c0, 1, 2, src1_ids)
    for group in pass_on:
        for copy in group:
            copy.wait_recv()

    def updated(rows, state, at, ids):
        grads = gsum[:, at] + summed(c0, 0, 0, ids)
        return adagrad(rows[...], state[0:1, :], grads)[0].astype(BF16)

    out_rows[1] = updated(req1, req1_st, slice(0, 256), req1_ids)
    rows_out1 = send(out_rows.at[1], rows_in.at[1], other)
    rows_out1.start()
    src1_b = updated(src1, src1_st, slice(256, 512), src1_ids)
    src1[...] = src1_b.astype(F32)
    queries = product(src1[...], rel1[...])
    queries_row, queries_b = queries.T.astype(BF16), queries.astype(BF16)

    def first_update(tile):
        at = slice(tile * GROUP, (tile + 1) * GROUP)
        grads = summed(c0, 0, 0, tile_ids(tile)) + summed(c0, 1, 2, tile_ids(tile))
        rows = tab[:, pl.ds(pl.multiple_of(own_first + tile * GROUP, GROUP), GROUP)]
        own[:, at], own_st[0:1, at] = adagrad(rows, own_st[0:1, at], grads)

    for tile in (0, 1):
        first_update(tile)

    rows_out1.wait_recv()
    backs1, shares1 = back_copies(1, c1, other, 1), share_copies(c1)
    coeffs = coefficients(queries_row, rows_in[1], live_s[1])
    d_queries = mat(rows_in[1], coeffs.T.astype(BF16))
    drel[1, :, 0:W] = conj_product(d_queries, src1[...]).T.astype(BF16)

    drel_sends[1].start()

    def quarter(ref, lo):
        return at_rows(ref, lo, FIRST_PART)

    my_lo = [lax.rem(first + k, 4) * FIRST_PART for k in (1, 2, 3, 0)]
    chains = range(CHAINS)
    firsts = [
        [
            send(at_rows(hsend, my_lo[k] + t * CHAIN, CHAIN), xin.at[k, pl.ds(t * CHAIN, CHAIN), :], first_peers[k])
            for k in range(3)
        ]
        for t in chains
    ]
    for lo in my_lo:
        quarter(h0, lo)[...] += relation_part(1, drel, msg[5:6, :], lo)
    drel_sends[1].wait_recv()
    for k in range(4):
        total = quarter(h0, my_lo[k])[...] + relation_part(1, dmate, comb[core_rep, 5:6, :], my_lo[k])
        if k < 3:
            quarter(hsend, my_lo[k])[...] = total.astype(BF16)
            firsts[0][k].start()
        else:
            qsum[...] = total
    start(firsts[1] + firsts[2])

    back[1] = mat(queries_b, coeffs.astype(BF16)).astype(BF16)
    c1[:, mine_at(0)] = conj_product(d_queries, rel1[...]).astype(BF16)

    for tile in (2, 3):
        first_update(tile)

    seconds = [
        [
            send(
                at_rows(qsend, t * CHAIN + lax.rem(second + k, 4) * THIRD_PART, THIRD_PART),
                sin.at[k - 1, pl.ds(t * THIRD_PART, THIRD_PART), :],
                second_peers[k - 1],
            )
            for k in range(1, 4)
        ]
        for t in chains
    ]
    for t in chains:
        at = slice(t * CHAIN, (t + 1) * CHAIN)
        total = qsum[at, :]
        for k in range(3):
            firsts[t][k].wait_recv()
            total = total + xin[k, at, :].astype(F32)
        qsum[at, :] = total
        qsend[at, :] = total.astype(BF16)
        start(seconds[t])
    start(backs1)
    for group in shares1[0]:
        start(group[:2])

    thirds = [
        send(at_rows(rsend, third(k)[1] * THIRD_PART, THIRD_PART), zin.at[k - 1], z_peers[k - 1])
        for k in range(1, 8)
    ]
    for t in chains:
        at = slice(t * THIRD_PART, (t + 1) * THIRD_PART)
        total = at_rows(qsum, t * CHAIN + second * THIRD_PART, THIRD_PART)[...]
        for k in range(3):
            seconds[t][k].wait_recv()
            total = total + sin[k, at, :].astype(F32)
        rsum[at, :] = total
        rsend[at, :] = total.astype(BF16)
        for k in range(1, 8):
            pl.when(holds(k, t))(thirds[k - 1].start)

    third_rows = at_rows(dall, third_row, THIRD_PART)
    out_z = [send(third_rows, third_rows, device) for device in z_peers]

    @pl.when(sums_third)
    def _():
        total = at_rows(rsum, my_third * THIRD_PART, THIRD_PART)[...]
        for k in range(7):
            thirds[k].wait_recv()
            total = total + zin[k].astype(F32)
        mean = jnp.sum(total * total, axis=1, keepdims=True) * (1.0 / W)
        delta = -RATE * total / (jnp.sqrt(rst[:, 0:1] + mean) + EPS)
        mean_hi = mean.astype(BF16).astype(F32)
        lane = iota((THIRD_PART, WIDE), 1)
        delta = jnp.where(lane == W, mean_hi, jnp.where(lane == W + 1, mean - mean_hi, delta))
        third_rows[...] = delta.astype(BF16)
        start(out_z)

    for k in range(len(PIECES)):
        backs1[k].wait_recv()
        start(shares1[1][k][:2])
        shares1[0][k][1].wait_recv()
        shares1[0][k][2].start()
    def own_tiles(tiles):
        for tile in tiles:
            at = slice(tile * GROUP, (tile + 1) * GROUP)
            grads = summed(c1, 0, 1, tile_ids(tile)) + summed(c1, 1, 3, tile_ids(tile))
            own[:, at], own_st[0:1, at] = adagrad(own[:, at], own_st[0:1, at], grads)

    out_second, out_first, swaps = [], [], []
    for t in chains:
        for k in range(1, 8):
            pl.when(holds(-k, t))(out_z[k - 1].wait_recv)
        rows = at_rows(dall, first_row + t * CHAIN + second * THIRD_PART, THIRD_PART)
        out_second.append([send(rows, rows, device) for device in second_peers])
        start(out_second[t])
    for group in shares1[1]:
        group[1].wait_recv()
        group[2].start()
    for t in chains:
        for copy in out_second[t]:
            copy.wait_recv()
        rows = at_rows(dall, first_row + t * CHAIN, CHAIN)
        out_first.append([send(rows, rows, device) for device in first_peers])
        start(out_first[t])
        swaps.append(send(rows, rows, core_mate))
        swaps[t].start()
    for kind in range(2):
        for group in shares1[kind]:
            group[0].wait_recv()
            group[2].wait_recv()
    own_tiles((0, 1, 2, 3))
    for k in range(8):
        est_ref[k : k + 1, :] = own_st[0:1, k * 128 : (k + 1) * 128]
    for t in chains:
        for k in range(3):
            out_first[t][k].wait_recv()
            rows = at_rows(dall, mine_from + lax.rem(first + 3 - k, 4) * FIRST_PART + t * CHAIN, CHAIN)
            swaps.append(send(rows, rows, core_mate))
            swaps[-1].start()

    def turn(lo, size):
        rows = dall[lo : lo + HALF_SLOTS, :].astype(F32).T[:, 0:size]
        rtab[:, lo : lo + size] = rtab[:, lo : lo + size] + rows[0:W]
        mean_ref[0:1, lo : lo + size] = rows[W : W + 1] + rows[W + 1 : W + 2]

    halves = ((0, HALF_SLOTS), (HALF_SLOTS, RELS - HALF_SLOTS))
    for c in range(2):
        pl.when(core == c)(functools.partial(turn, *halves[c]))
    for copy in swaps:
        copy.wait_recv()
    for c in range(2):
        pl.when(core == c)(functools.partial(turn, *halves[1 - c]))

    for copy in [ask0, ask1, rows_out0, rows_out1] + combs + backs0 + backs0_y + backs1 + drel_sends:
        copy.wait_send()
    for group in shares0 + pass_on + shares1[0] + shares1[1]:
        for copy in group:
            copy.wait_send()
    for group in firsts + seconds + out_second + out_first + [swaps]:
        for copy in group:
            copy.wait_send()
    for k in range(1, 8):
        pl.when(third(k)[0])(thirds[k - 1].wait_send)

    @pl.when(sums_third)
    def _():
        for copy in out_z:
            copy.wait_send()


OWN_PIECES = ((0, 104), (104, 104), (208, 96), (304, 96))


def finish(own, own_state, relations, mean, rstate, ent_hbm, est_ref, rel_hbm, nstate, sem):
    stores = [
        pltpu.make_async_copy(source.at[pl.ds(lo, size), :], target.at[pl.ds(lo, size), :], sem.at[first + k])
        for source, target, first in ((own, ent_hbm, 0), (relations, rel_hbm, 4))
        for k, (lo, size) in enumerate(OWN_PIECES)
    ]
    for store in stores:
        store.start()
    est_ref[...] = own_state[...]
    nstate[...] = rstate[...] + mean[0:1, :].reshape(SLOTS)[:RELS]
    for store in stores:
        store.wait()


def per_device(
    entity_table, entity_state, relation_table, relation_state, source_rows, target_rows, relation_ids, live_counts
):
    vmem, ids = pl.BlockSpec(memory_space=pltpu.VMEM), pltpu.VMEM((2, 1, GROUP), I32)
    anywhere = pl.BlockSpec(memory_space=pl.ANY)
    contributions = pltpu.VMEM((W, 8 * GROUP), BF16)
    blocks = pltpu.VMEM((2, W, GROUP), BF16)
    block_f, state_row = pltpu.VMEM((W, GROUP), F32), pltpu.VMEM((8, GROUP), F32)
    own, own_state, new_relations, mean = pl.pallas_call(
        kernel,
        out_shape=(
            pltpu.VMEM((W, SHARE), F32),
            pltpu.VMEM((8, 128), F32),
            pltpu.VMEM((W, RELS), F32),
            pltpu.VMEM((8, SLOTS), F32),
        ),
        in_specs=[anywhere] * 8,
        out_specs=(vmem, vmem, vmem, vmem),
        scratch_shapes=[
            pltpu.VMEM((W, ROWS), F32),
            pltpu.VMEM((W + 16, ROWS), BF16),
            pltpu.VMEM((W, RELS), BF16),
            pltpu.VMEM((16, ROWS), F32),
            pltpu.VMEM((ROWS // 128, 128), F32),
            pltpu.SMEM((RELS,), F32),
            ids, ids, ids,
            pltpu.SMEM((2,), I32),
            pltpu.VMEM((8, GROUP), I32),
            pltpu.VMEM((2, 8, GROUP), I32),
            pltpu.VMEM((4, 8, GROUP), I32),
            pltpu.VMEM((4, 4 * GROUP, 1), F32),
            blocks, blocks, blocks,
            contributions, contributions,
            pltpu.VMEM((W, 2 * GROUP), F32),
            block_f, block_f, state_row, state_row, block_f,
            pltpu.VMEM((2, GROUP, WIDE), BF16),
            pltpu.VMEM((8, SHARE), F32),
            pltpu.VMEM((HALF_SLOTS, WIDE), F32),
            pltpu.VMEM((HALF_SLOTS, WIDE), BF16),
            pltpu.VMEM((2, GROUP, WIDE), BF16),
            pltpu.VMEM((3, FIRST_PART, WIDE), BF16),
            pltpu.VMEM((FIRST_PART, WIDE), F32),
            pltpu.VMEM((FIRST_PART, WIDE), BF16),
            pltpu.VMEM((3, CHAINS * THIRD_PART, WIDE), BF16),
            pltpu.VMEM((CHAINS * THIRD_PART, WIDE), F32),
            pltpu.VMEM((CHAINS * THIRD_PART, WIDE), BF16),
            pltpu.VMEM((7, THIRD_PART, WIDE), BF16),
            pltpu.VMEM((THIRD_PART, 128), F32),
            pltpu.VMEM((SLOTS, WIDE), BF16),
            pltpu.SemaphoreType.DMA((11,)),
            pltpu.SemaphoreType.DMA((SEMS,)),
            pltpu.SemaphoreType.DMA((SEMS,)),
        ],
        compiler_params=pltpu.CompilerParams(
            collective_id=0, has_side_effects=True, vmem_limit_bytes=58 * 1024 * 1024
        ),
    )(
        entity_table.T, relation_table.T, entity_state.reshape(ROWS // 128, 128), relation_state,
        source_rows, target_rows, relation_ids, live_counts.reshape(-1),
    )
    own, own_state, new_relations, new_state = pl.pallas_call(
        finish,
        out_shape=(
            jax.ShapeDtypeStruct((W, SHARE), F32),
            jax.ShapeDtypeStruct((8, 128), F32),
            jax.ShapeDtypeStruct((W, RELS), F32),
            jax.ShapeDtypeStruct((RELS,), F32),
        ),
        in_specs=[vmem, vmem, vmem, vmem, vmem],
        out_specs=(anywhere, vmem, anywhere, vmem),
        scratch_shapes=[
            pltpu.SemaphoreType.DMA((8,)),
        ],
        compiler_params=pltpu.CompilerParams(vmem_limit_bytes=12 * 1024 * 1024),
    )(own, own_state, new_relations, mean, relation_state)
    return own.T, own_state.reshape(-1), new_relations.T, new_state


def solution(mesh):
    in_specs = (
        P("dom", None),
        P("dom"),
        P(),
        P(),
        P(None, "dom", "rep"),
        P(None, "dom", "rep"),
        P(None, "dom", "rep"),
        P(None, "dom", "rep"),
    )
    out_specs = (P(("dom", "rep"), None), P(("dom", "rep")), P(), P())
    return jax.shard_map(per_device, mesh=mesh, in_specs=in_specs, out_specs=out_specs, check_vma=False)
```
